128 devices in a mesh: dp: 16 (over y, x_hi, core), tensor: 8 (over z, x_lo).
Axes of the slice: x: 4 (x_hi: 2, x_lo: 2; x = x_hi * 2 + x_lo), y: 4, z: 4, core: 2. Of those that a mesh axis runs over, the one named last changes fastest.
Arguments:
- tokens: bfloat16 [8192, 4096], P(('dp', 'tensor')), may hold values from -24 to 24
- w_up: bfloat16 [4096, 8192], P(None, 'tensor'), may hold values from -0.125 to 0.125
- w_down: bfloat16 [8192, 4096], P('tensor'), may hold values from -0.09375 to 0.09375
- mask_up: int32 [64, 128], P(None, 'tensor'), may hold values from 0 to 1, as said below
- mask_down: int32 [128, 64], P('tensor'), may hold values from 0 to 1, as said below
- cotangent: bfloat16 [8192, 4096], P(('dp', 'tensor')), may hold values from -24 to 24
Outputs:
- output: bfloat16 [8192, 4096], P(('dp', 'tensor'))
- grad_tokens: bfloat16 [8192, 4096], P(('dp', 'tensor'))
- grad_up: float32 [4096, 8192], P('dp', 'tensor')
- grad_down: float32 [8192, 4096], P('tensor', 'dp')
The draws below stay inside these ranges and needn't reach their ends.
Inputs may be any that keep to these rules, and one draw needn't show every extreme that they name: `mask_up`: split into aligned groups of 4 block rows by 16 block columns, every group keeps at most 40 blocks, and some group keeps exactly 40. `mask_down`: split into aligned groups of 16 block rows by 4 block columns, every group keeps at most 40 blocks, and some group keeps exactly 40.
All inputs are finite; a program needn't handle non-finite values.
Results may differ from the reference program's by a relative error of at most 0.019.
Values may be sent and summed in bfloat16 or wider, within the bound.
No kernel may reach another device: no remote copies, remote signals or barrier semaphores. Data moves between devices by JAX's collectives and lax.ppermute only.
A program may use at most 256 MiB of HBM per device.

```python
import math
import jax
import jax.numpy as jnp
from jax import lax

D = 4096
FFW = 8192
B = 64
TOKENS = 8192
ROWS = 512
N_DP = 16
N_TENSOR = 8


def sparse_blocks(key, group_rows, group_cols, rows, cols):
    total = rows * cols
    groups = group_rows * group_cols
    key_count, key_top, key_rank = jax.random.split(key, 3)
    counts = jax.random.randint(key_count, (groups,), total * 3 // 8, total * 5 // 8 + 1)
    top = jax.random.randint(key_top, (), 0, groups)
    counts = jnp.where(jnp.arange(groups) == top, total * 5 // 8, counts)
    ranks = jax.vmap(lambda k: jax.random.permutation(k, total))(jax.random.split(key_rank, groups))
    keep = (ranks < counts[:, None]).astype(jnp.int32)
    keep = keep.reshape(group_rows, group_cols, rows, cols).transpose(0, 2, 1, 3)
    return keep.reshape(group_rows * rows, group_cols * cols)


def draw_mask_up(key, part):
    return sparse_blocks(jax.random.fold_in(key, 11), N_DP, N_TENSOR, D // (N_DP * B), FFW // (N_TENSOR * B))


def draw_mask_down(key, part):
    return sparse_blocks(jax.random.fold_in(key, 23), N_TENSOR, N_DP, FFW // (N_TENSOR * B), D // (N_DP * B))


def raised(array, stream_key, source, target, blocks, factor):
    owner, partner = [(jnp.arange(array.shape[axis_at]) // (array.shape[axis_at] // blocks)).reshape([-1 if axis == axis_at else 1 for axis in range(array.ndim)]) for axis_at in (source, target)]
    chosen = jax.random.permutation(stream_key, blocks)[partner]
    strong = (owner == chosen) | (owner == (partner + blocks // 2) % blocks)
    return jnp.where(strong, factor * array, array)


def steps_of(own_key, extent, cuts, least, top_value):
    level, own = 1.0, jax.random.fold_in(own_key, 6)
    for position, parts in cuts:
        draws = jnp.exp(jax.random.uniform(jax.random.fold_in(own, position), (parts,), jnp.float32, least / len(cuts), top_value / len(cuts)))
        level = level * jnp.repeat(draws, extent[position] // parts).reshape([-1 if axis == position else 1 for axis in range(len(extent))])
    return level


def noise(stream_key, shape, width, most, cuts=(), kind=jnp.bfloat16):
    gain = steps_of(stream_key, shape, cuts, -0.22, 0.18) if cuts else 1.0
    entries = jax.random.normal(stream_key, shape, jnp.float32) * width * gain
    return jnp.minimum(jnp.maximum(entries, -most), most).astype(kind)


def gaussian_with(key, extent, scale, reach, pieces, heavy, kind=jnp.bfloat16):
    array = scale * jax.random.normal(key, extent, jnp.float32)
    if pieces:
        array = array * steps_of(key, extent, pieces, -0.22, 0.18)
    return jnp.clip(raised(array, jax.random.fold_in(key, 3), *heavy), -reach, reach).astype(kind)


def setup_inputs(seed: int = 0) -> dict:
    key_list = jax.random.split(jax.random.key(seed), 7)
    tokens = gaussian_with(key_list[0], (TOKENS, D), 1.0, 24.0, ((0, 128),), (0, 1, 128, 5.5))
    w_up = noise(key_list[1], (D, FFW), (D // 2) ** -0.5, 0.125, ((1, 8),))
    w_down = noise(key_list[2], (FFW, D), (FFW // 2) ** -0.5, 0.09375, ((0, 8),))
    mask_up = draw_mask_up(jax.random.fold_in(key_list[6], 71), 0)
    mask_down = draw_mask_down(jax.random.fold_in(key_list[6], 71), 0)
    cotangent = gaussian_with(key_list[5], (TOKENS, D), 1.0, 24.0, ((0, 128),), (0, 1, 128, 5.5))
    return {"tokens": tokens, "w_up": w_up, "w_down": w_down, "mask_up": mask_up, "mask_down": mask_down, "cotangent": cotangent}


def gelu_tanh(value):
    inner = math.sqrt(2.0 / math.pi) * (value + 0.044715 * value * value * value)
    return 0.5 * value * (1.0 + jnp.tanh(inner))

def gelu_slope(value):
    coeff = math.sqrt(2.0 / math.pi)
    tanh_part = jnp.tanh(coeff * (value + 0.044715 * value * value * value))
    return 0.5 * (1.0 + tanh_part) + 0.5 * value * (1.0 - tanh_part * tanh_part) * coeff * (1.0 + 3.0 * 0.044715 * value * value)

def expand_mask(mask):
    return jnp.repeat(jnp.repeat(mask, B, axis=0), B, axis=1)

def group_sum(left, right, keep):
    left_groups = left.reshape(N_DP, ROWS, left.shape[1])
    right_groups = right.reshape(N_DP, ROWS, right.shape[1])

    def step(total, pair):
        part = jnp.dot(pair[0].T, pair[1], preferred_element_type=jnp.float32) * keep
        rounded = lax.optimization_barrier(part.astype(jnp.bfloat16))
        return (total + rounded.astype(jnp.float32), None)
    init = jnp.zeros((left.shape[1], right.shape[1]), jnp.float32)
    total, unused = lax.scan(step, init, (left_groups, right_groups))
    return total

def reference(tokens, w_up, w_down, mask_up, mask_down, cotangent):
    keep_up = expand_mask(mask_up)
    keep_down = expand_mask(mask_down)
    up_kept = w_up * keep_up.astype(w_up.dtype)
    down_kept = w_down * keep_down.astype(w_down.dtype)
    pre = jnp.dot(tokens, up_kept, preferred_element_type=jnp.float32)
    hidden = gelu_tanh(pre).astype(jnp.bfloat16)
    output = jnp.dot(hidden, down_kept, preferred_element_type=jnp.float32).astype(jnp.bfloat16)
    grad_hidden = jnp.dot(cotangent, down_kept.T, preferred_element_type=jnp.float32)
    grad_pre = (grad_hidden * gelu_slope(pre)).astype(jnp.bfloat16)
    grad_tokens = jnp.dot(grad_pre, up_kept.T, preferred_element_type=jnp.float32).astype(jnp.bfloat16)
    grad_up = group_sum(tokens, grad_pre, keep_up.astype(jnp.float32))
    grad_down = group_sum(hidden, cotangent, keep_down.astype(jnp.float32))
    return (output, grad_tokens, grad_up, grad_down)
```

```python
import functools
import math

import jax
import jax.numpy as jnp
from jax import lax
from jax.experimental import pallas as pl
from jax.experimental.pallas import tpu as pltpu
from jax.sharding import PartitionSpec as P

B = 64
D = 4096
F = 1024
KEPT = 40
SLAB = KEPT // 2 * B
MIB = 1 << 20
C = math.sqrt(2.0 / math.pi)
f32, bf16 = jnp.float32, jnp.bfloat16
AXES = ("dp", "tensor")


def device_at(x, y, z, c):
    x, y, z = x % 4, y % 4, z % 4
    return ((y * 2 + x // 2) * 2 + c) * 8 + z * 2 + x % 2


def shift(value, dx=0, dy=0, dz=0, dc=0):
    pairs = [
        (device_at(x, y, z, c), device_at(x + dx, y + dy, z + dz, c ^ dc))
        for x in range(4)
        for y in range(4)
        for z in range(4)
        for c in range(2)
    ]
    return lax.ppermute(value, AXES, pairs)


def cost(flops, nbytes):
    return pl.CostEstimate(flops=int(flops), bytes_accessed=int(nbytes), transcendentals=0)


def spread(blocks):
    row = lax.broadcasted_iota(jnp.int32, (blocks, blocks * B), 0)
    col = lax.broadcasted_iota(jnp.int32, (blocks, blocks * B), 1)
    return (row == col // B).astype(f32).astype(bf16)


def mask_kernel(mu, md, wu, wd, uk, dk, su, sd):
    i = pl.program_id(0)

    @pl.when(i == 0)
    def _():
        su[...] = jnp.dot(mu[...].astype(f32).astype(bf16), spread(16), preferred_element_type=f32)
        sd[...] = jnp.dot(md[...].astype(f32).astype(bf16), spread(64), preferred_element_type=f32)

    for k in range(4):
        row = su[pl.ds(4 * i + k, 1), :]
        block = wu[k * B : (k + 1) * B, :]
        uk[k * B : (k + 1) * B, :] = (block.astype(f32) * row).astype(bf16)
    dk[...] = (wd[...].astype(f32) * sd[pl.ds(i, 1), :]).astype(bf16)


def kept_weights(w_up, w_down, mask_up, mask_down):
    return pl.pallas_call(
        mask_kernel,
        grid=(16,),
        in_specs=[
            pl.BlockSpec((64, 16), lambda i: (0, 0)),
            pl.BlockSpec((16, 64), lambda i: (0, 0)),
            pl.BlockSpec((256, F), lambda i: (i, 0)),
            pl.BlockSpec((64, D), lambda i: (i, 0)),
        ],
        out_specs=[
            pl.BlockSpec((256, F), lambda i: (i, 0)),
            pl.BlockSpec((64, D), lambda i: (i, 0)),
        ],
        out_shape=[jax.ShapeDtypeStruct((D, F), bf16), jax.ShapeDtypeStruct((F, D), bf16)],
        scratch_shapes=[pltpu.VMEM((64, F), f32), pltpu.VMEM((16, D), f32)],
        compiler_params=pltpu.CompilerParams(vmem_limit_bytes=24 * MIB),
        cost_estimate=cost(0, 36 * MIB),
        name="kept_weights",
    )(mask_up, mask_down, w_up, w_down)


def front_kernel(copies, n_pieces, *refs):
    pieces = refs[:n_pieces]
    uk, dk, hid, gp, hid_t, gp_t, xf, df, sem = refs[n_pieces:]

    @pl.when(pl.program_id(0) == 0)
    def _():
        moves = [
            pltpu.make_async_copy(
                pieces[p].at[pl.ds(src, n), :], (xf, df)[to].at[pl.ds(dst, n), :], sem.at[k]
            )
            for k, (p, src, n, to, dst) in enumerate(copies)
        ]
        for move in moves:
            move.start()
        for move in moves:
            move.wait()

    pre = jnp.dot(xf[...], uk[...], preferred_element_type=f32)
    back = lax.dot_general(df[...], dk[...], (((1,), (1,)), ((), ())), preferred_element_type=f32)
    t = jnp.tanh(C * (pre + 0.044715 * pre * pre * pre))
    h = 0.5 * pre * (1.0 + t)
    slope = 0.5 * (1.0 + t) + 0.5 * pre * (1.0 - t * t) * C * (1.0 + 3.0 * 0.044715 * pre * pre)
    g = back * slope
    hid[...] = h.astype(bf16)
    gp[...] = g.astype(bf16)
    hid_t[...] = h.T.astype(bf16)
    gp_t[...] = g.T.astype(bf16)


def front(pieces, copies, up_kept, down_kept):
    n, tile = len(pieces), 256
    any_spec = pl.BlockSpec(memory_space=pl.ANY)
    whole = pl.BlockSpec((256, D), lambda i: (0, 0))
    across = pl.BlockSpec((256, tile), lambda i: (0, i))
    down = pl.BlockSpec((tile, 256), lambda i: (i, 0))
    return pl.pallas_call(
        functools.partial(front_kernel, copies, n),
        grid=(F // tile,),
        in_specs=[any_spec] * n
        + [pl.BlockSpec((D, tile), lambda i: (0, i)), pl.BlockSpec((tile, D), lambda i: (i, 0))],
        out_specs=[across, across, down, down, whole, whole],
        out_shape=[
            jax.ShapeDtypeStruct((256, F), bf16),
            jax.ShapeDtypeStruct((256, F), bf16),
            jax.ShapeDtypeStruct((F, 256), bf16),
            jax.ShapeDtypeStruct((F, 256), bf16),
            jax.ShapeDtypeStruct((256, D), bf16),
            jax.ShapeDtypeStruct((256, D), bf16),
        ],
        scratch_shapes=[pltpu.SemaphoreType.DMA((len(copies),))],
        compiler_params=pltpu.CompilerParams(vmem_limit_bytes=40 * MIB),
        cost_estimate=cost(4 * 256 * D * F, 26 * MIB),
        name="front",
    )(*pieces, up_kept, down_kept)


COLUMN = (
    (0, 0, 64, 0, 0),
    (1, 0, 64, 0, 64),
    (2, 0, 64, 0, 128),
    (6, 0, 32, 0, 192),
    (7, 0, 32, 0, 224),
    (3, 0, 64, 1, 0),
    (4, 0, 64, 1, 64),
    (5, 0, 64, 1, 128),
    (6, 32, 32, 1, 192),
    (7, 32, 32, 1, 224),
)
SIDE = tuple(
    (p + 4 * s, src, n, to, dst + 128 * s)
    for s in range(2)
    for p, src, n, to, dst in (
        (0, 0, 32, 0, 0),
        (1, 0, 64, 0, 32),
        (3, 0, 32, 0, 96),
        (0, 32, 32, 1, 0),
        (2, 0, 64, 1, 32),
        (3, 32, 32, 1, 96),
    )
)


def shares(hid, gp, uk, dk):
    o = jnp.dot(hid[...], dk[...], preferred_element_type=f32).astype(bf16)
    t = lax.dot_general(
        gp[...], uk[...], (((1,), (1,)), ((), ())), preferred_element_type=f32
    ).astype(bf16)
    return o, t


def column_kernel(hid, gp, uk, dk, o_ref, t_ref):
    o_ref[...], t_ref[...] = shares(hid, gp, uk, dk)


def side_kernel(hid, gp, uk, dk, *outs):
    o, t = shares(hid, gp, uk, dk)
    for s in range(2):
        q1, q2, q3, q4 = outs[4 * s : 4 * s + 4]
        a = 128 * s
        q1[0:32, :], q1[32:64, :] = o[a + 96 : a + 128, :], t[a + 96 : a + 128, :]
        q2[...] = o[a + 32 : a + 96, :]
        q3[...] = t[a + 32 : a + 96, :]
        q4[0:32, :], q4[32:64, :] = o[a : a + 32, :], t[a : a + 32, :]


def back_shares(kernel, n_out, rows, hid, gp, up_kept, down_kept):
    tile = 512
    return pl.pallas_call(
        kernel,
        grid=(D // tile,),
        in_specs=[
            pl.BlockSpec((256, F), lambda i: (0, 0)),
            pl.BlockSpec((256, F), lambda i: (0, 0)),
            pl.BlockSpec((tile, F), lambda i: (i, 0)),
            pl.BlockSpec((F, tile), lambda i: (0, i)),
        ],
        out_specs=[pl.BlockSpec((rows, tile), lambda i: (0, i))] * n_out,
        out_shape=[jax.ShapeDtypeStruct((rows, D), bf16)] * n_out,
        compiler_params=pltpu.CompilerParams(vmem_limit_bytes=24 * MIB),
        cost_estimate=cost(4 * 256 * D * F, 22 * MIB),
        name="shares",
    )(hid, gp, up_kept, down_kept)


def packed_kernel(groups, blocks, a1, a2, b1, b2, out, t):
    j = groups[pl.program_id(0)]
    for r in range(0, F, 256):
        rows = slice(r, r + 256)
        acc = jnp.dot(a1[rows, :], b1[...], preferred_element_type=f32)
        acc += jnp.dot(a2[rows, :], b2[...], preferred_element_type=f32)
        for ct in range(2):
            part = acc[:, ct * 128 : (ct + 1) * 128]
            t[ct, rows, :] = part.astype(bf16)
            t[2 + ct, rows, :] = pltpu.roll(part, 64, 1).astype(bf16)
    for p in range(KEPT // 2):
        ia, ib = blocks[j, 2 * p], blocks[j, 2 * p + 1]
        ra = pl.multiple_of((ia // 4) * B, B)
        rb = pl.multiple_of((ib // 4) * B, B)
        va = (ia % 2) * 2 + (ia % 4) // 2
        vb = (1 - ib % 2) * 2 + (ib % 4) // 2
        to = slice(p * B, (p + 1) * B)
        out[0, to, 0:B] = t[va, pl.ds(ra, B), 0:B]
        out[0, to, B : 2 * B] = t[vb, pl.ds(rb, B), B : 2 * B]


def packed(groups, blocks, a1, a2, b1, b2):
    left = pl.BlockSpec((F, 256), lambda j, g, k: (0, 0))
    right = pl.BlockSpec((256, 256), lambda j, g, k: (0, g[j]))
    return pl.pallas_call(
        packed_kernel,
        grid_spec=pltpu.PrefetchScalarGridSpec(
            num_scalar_prefetch=2,
            grid=(8,),
            in_specs=[left, left, right, right],
            out_specs=pl.BlockSpec((1, SLAB, 128), lambda j, g, k: (j, 0, 0)),
            scratch_shapes=[pltpu.VMEM((4, F, 128), bf16)],
        ),
        out_shape=jax.ShapeDtypeStruct((8, SLAB, 128), bf16),
        compiler_params=pltpu.CompilerParams(vmem_limit_bytes=24 * MIB),
        cost_estimate=cost(2 * 512 * F * 2048, 6 * MIB),
        name="packed",
    )(groups, blocks, a1, a2, b1, b2)


def expand_kernel(turned, places, w, f, out, s, dense):
    total = w[0].astype(f32) + f[0].astype(f32)
    s[0] = total
    s[1] = pltpu.roll(total, 64, 1)
    target = dense if turned else out
    for r in range(16):
        rows = slice(r * B, (r + 1) * B)
        for c in range(4):
            slot = places[r * 4 + c]
            at = jnp.maximum(slot, 0)
            row = pl.multiple_of((at // 2) * B, B)
            half = slice((c % 2) * B, (c % 2 + 1) * B)
            version = at % 2 if c % 2 == 0 else 1 - at % 2
            block = s[version, pl.ds(row, B), half]
            target[rows, c * B : (c + 1) * B] = jnp.where(slot >= 0, block, 0.0)
    if turned:
        for r in range(0, F, 128):
            for c in range(0, 256, 128):
                out[c : c + 128, r : r + 128] = dense[r : r + 128, c : c + 128].T


def expand(turned, places, w, f):
    slab = pl.BlockSpec((1, SLAB, 128), lambda i, p: (0, 0, 0))
    shape = (256, F) if turned else (F, 256)
    return pl.pallas_call(
        functools.partial(expand_kernel, turned),
        grid_spec=pltpu.PrefetchScalarGridSpec(
            num_scalar_prefetch=1,
            grid=(1,),
            in_specs=[slab, slab],
            out_specs=pl.BlockSpec(shape, lambda i, p: (0, 0)),
            scratch_shapes=[pltpu.VMEM((2, SLAB, 128), f32), pltpu.VMEM((F, 256), f32)],
        ),
        out_shape=jax.ShapeDtypeStruct(shape, f32),
        compiler_params=pltpu.CompilerParams(vmem_limit_bytes=24 * MIB),
        cost_estimate=cost(0, 2 * MIB),
        name="expand",
    )(places, w, f)


def plan(mask_up, mask_down):
    up = mask_up.reshape(16, 4, 16).transpose(0, 2, 1).reshape(16, 64)
    down = mask_down.reshape(16, 16, 4).transpose(1, 0, 2).reshape(16, 64)
    keep = (jnp.stack([up, down]) != 0).astype(jnp.int32)
    place = jnp.arange(64, dtype=jnp.int32)
    slot = jnp.sum(keep[:, :, None, :] * (place[None, :] < place[:, None]), axis=-1)
    wanted = jnp.arange(KEPT, dtype=jnp.int32)
    hit = (slot[:, :, None, :] == wanted[:, None]) & (keep[:, :, None, :] != 0)
    blocks = jnp.sum(jnp.where(hit, place, 0), axis=-1)
    places = jnp.where(keep != 0, slot, -1)
    return blocks, places


def add(*terms):
    total = terms[0].astype(f32)
    for term in terms[1:]:
        total = total + term.astype(f32)
    return total.astype(bf16)


def cat(*parts):
    return jnp.concatenate(parts, axis=0)


def dp_sum(mine, theirs):
    got = shift(theirs, dc=1)
    v = [add(mine[k : k + 1], got[k : k + 1]) for k in (0, 1)]
    low, high = shift(v[0], dy=1), shift(v[1], dy=-1)
    ahead = cat(add(mine[2:3], got[2:3], low), add(mine[3:4], got[3:4]))
    behind = cat(add(mine[4:5], got[4:5]), add(mine[5:6], got[5:6], high))
    from_behind, from_ahead = shift(ahead, dy=1), shift(behind, dy=-1)
    far = add(mine[7:8], got[7:8], from_behind[1:2], from_ahead[1:2])
    near = add(mine[6:7], got[6:7], from_behind[0:1], from_ahead[0:1])
    return near, shift(far, dx=2)


def local(tokens, w_up, w_down, mask_up, mask_down, cotangent):
    x, d = tokens, cotangent
    dp = lax.axis_index("dp")
    y, xh, c = dp // 4, (dp // 2) % 2, dp % 2

    xm, xp = shift(x, dz=1), shift(x, dz=-1)
    l1, r1 = shift(cat(x[:32], d[:32]), dx=1), shift(cat(x[32:], d[32:]), dx=-1)
    dm, dp_ = shift(d, dz=1), shift(d, dz=-1)
    l2 = shift(cat(xm[:32], xp[:32]), dx=1)
    r2 = shift(cat(xm[32:], xp[32:]), dx=-1)
    two_a = shift(cat(xm[:32], dm[:32]), dz=1)
    two_b = shift(cat(xp[32:], dp_[32:]), dz=-1)
    l3 = shift(cat(dm[:32], dp_[:32]), dx=1)
    r3 = shift(cat(dm[32:], dp_[32:]), dx=-1)
    l4, r4 = shift(two_a, dx=1), shift(two_b, dx=-1)

    uk, dk = kept_weights(w_up, w_down, mask_up, mask_down)
    blocks, places = plan(mask_up, mask_down)
    order = [(2, 0), (2, 1), (1, 0), (1, 1), (3, 0), (3, 1), (0, 0), (0, 1)]
    near = jnp.stack([((y + dy) % 4) * 4 + (xh ^ e) * 2 + c for dy, e in order]).astype(jnp.int32)
    away = near ^ 1
    own = lax.dynamic_index_in_dim(places, dp, 1, keepdims=False)

    hid1, gp1, hid1_t, gp1_t, x1, d1 = front(
        [x, xm, xp, d, dm, dp_, two_a, two_b], COLUMN, uk, dk
    )
    o_col, t_col = back_shares(column_kernel, 2, 256, hid1, gp1, uk, dk)
    hid2, gp2, hid2_t, gp2_t, x2, d2 = front([l1, l2, l3, l4, r1, r2, r3, r4], SIDE, uk, dk)

    up_away = packed(away, blocks[0], gp1_t, gp2_t, x1, x2)
    up_near = packed(near, blocks[0], gp1_t, gp2_t, x1, x2)
    side = back_shares(side_kernel, 8, 64, hid2, gp2, uk, dk)
    down_away = packed(away, blocks[1], hid1_t, hid2_t, d1, d2)
    down_near = packed(near, blocks[1], hid1_t, hid2_t, d1, d2)

    a1, a2, a3, a4 = (shift(v, dx=-1) for v in side[:4])
    b1, b2, b3, b4 = (shift(v, dx=1) for v in side[4:])
    za = shift(cat(add(o_col[192:224], a1[:32]), add(t_col[192:224], a1[32:])), dz=1)
    zb = shift(cat(add(o_col[224:256], b1[:32]), add(t_col[224:256], b1[32:])), dz=-1)

    def along_z(col, a, b, za, zb):
        p = cat(add(col[128:160], a[32:], za), add(col[160:192], b[32:]))
        m = cat(add(col[64:96], a[:32]), add(col[96:128], b[:32], zb))
        return shift(p, dz=1), shift(m, dz=-1)

    o_p, o_m = along_z(o_col, a2, b2, za[:32], zb[:32])
    t_p, t_m = along_z(t_col, a3, b3, za[32:], zb[32:])
    output = add(o_col[:64], cat(a4[:32], b4[:32]), o_p, o_m)
    grad_tokens = add(t_col[:64], cat(a4[32:], b4[32:]), t_p, t_m)

    grad_up = expand(True, own[0], *dp_sum(up_near, up_away))
    grad_down = expand(False, own[1], *dp_sum(down_near, down_away))
    return output, grad_tokens, grad_up, grad_down


def solution(mesh):
    placed = (
        P(("dp", "tensor"), None),
        P(None, "tensor"),
        P("tensor", None),
        P(None, "tensor"),
        P("tensor", None),
        P(("dp", "tensor"), None),
    )
    return jax.shard_map(
        local,
        mesh=mesh,
        in_specs=placed,
        out_specs=(
            P(("dp", "tensor"), None),
            P(("dp", "tensor"), None),
            P("dp", "tensor"),
            P("tensor", "dp"),
        ),
        check_vma=False,
    )
```

```python
import functools
import math

import jax
import jax.numpy as jnp
from jax import lax
from jax.experimental import pallas as pl
from jax.experimental.pallas import tpu as pltpu
from jax.sharding import PartitionSpec as P

B = 64
D = 4096
F = 1024
KEPT = 40
SLAB = KEPT // 2 * B
MIB = 1 << 20
VMEM = 60 * MIB
C = math.sqrt(2.0 / math.pi)
f32, bf16 = jnp.float32, jnp.bfloat16
AXES = ("dp", "tensor")


def device_at(x, y, z, c):
    x, y, z = x % 4, y % 4, z % 4
    return ((y * 2 + x // 2) * 2 + c) * 8 + z * 2 + x % 2


def send(value, to):
    pairs = [
        (device_at(x, y, z, c), device_at(*to(x, y, z, c)))
        for x in range(4)
        for y in range(4)
        for z in range(4)
        for c in range(2)
    ]
    return lax.ppermute(value, AXES, pairs)


def shift(value, dx=0, dz=0):
    return send(value, lambda x, y, z, c: (x + dx, y, z + dz, c))


def to_core(value):
    return send(value, lambda x, y, z, c: (x, y, z, 1 - c))


def to_pair(value):
    return send(value, lambda x, y, z, c: (x, y ^ 1, z, c))


def to_mirror(value):
    return send(value, lambda x, y, z, c: (x, 3 - y, z, c))


def cost(flops, nbytes):
    return pl.CostEstimate(flops=int(flops), bytes_accessed=int(nbytes), transcendentals=0)


def spread(blocks):
    row = lax.broadcasted_iota(jnp.int32, (blocks, blocks * B), 0)
    col = lax.broadcasted_iota(jnp.int32, (blocks, blocks * B), 1)
    return (row == col // B).astype(f32).astype(bf16)


def mask_kernel(blocks, per, mask, w, *rest):
    kept, rows = rest[-2:]
    i = pl.program_id(0)

    @pl.when(i == 0)
    def _():
        rows[...] = jnp.dot(
            mask[...].astype(f32).astype(bf16), spread(blocks), preferred_element_type=f32
        )

    for k in range(per):
        at = slice(k * B, (k + 1) * B)
        kept[at, :] = (w[at, :].astype(f32) * rows[pl.ds(per * i + k, 1), :]).astype(bf16)


def kept_weight(w, mask, *ready):
    rows, cols = w.shape
    steps = 4
    block = pl.BlockSpec((rows // steps, cols), lambda i: (i, 0))
    return pl.pallas_call(
        functools.partial(mask_kernel, cols // B, rows // B // steps),
        grid=(steps,),
        in_specs=[pl.BlockSpec(mask.shape, lambda i: (0, 0)), block]
        + [pl.BlockSpec(memory_space=pl.ANY)] * len(ready),
        out_specs=block,
        out_shape=jax.ShapeDtypeStruct((rows, cols), bf16),
        scratch_shapes=[pltpu.VMEM((rows // B, cols), f32)],
        compiler_params=pltpu.CompilerParams(vmem_limit_bytes=VMEM),
        cost_estimate=cost(0, 18 * MIB),
        name="kept_weight",
    )(mask, w, *ready)


TOKENS_COLUMN = ((0, 0, 64, 0), (1, 0, 64, 64), (2, 0, 64, 128), (3, 0, 32, 192), (4, 0, 32, 224))
TOKENS_SIDE = tuple(
    (3 * s + p, 0, n, 128 * s + dst) for s in range(2) for p, n, dst in ((0, 32, 0), (1, 64, 32), (2, 32, 96))
)
COTANGENTS = (
    (0, 0, 64, 0),
    (1, 32, 64, 64),
    (2, 32, 64, 128),
    (3, 0, 32, 192),
    (4, 0, 32, 224),
    (5, 32, 32, 256),
    (6, 32, 64, 288),
    (7, 0, 32, 352),
    (8, 32, 32, 384),
    (9, 32, 64, 416),
    (10, 0, 32, 480),
)
ANY = pl.BlockSpec(memory_space=pl.ANY)


def collect(table, pieces, rows, sem, out, row, out_sem):
    i = pl.program_id(0)
    keep = pltpu.make_async_copy(rows, out.at[pl.ds(row, rows.shape[0]), :], out_sem)

    @pl.when(i == 0)
    def _():
        moves = [
            pltpu.make_async_copy(pieces[p].at[pl.ds(src, n), :], rows.at[pl.ds(dst, n), :], sem.at[k])
            for k, (p, src, n, dst) in enumerate(table)
        ]
        for move in moves:
            move.start()
        for move in moves:
            move.wait()
        keep.start()

    def finish():
        @pl.when(i == pl.num_programs(0) - 1)
        def _():
            keep.wait()

    return finish


def hidden_kernel(table, n_pieces, half, *refs):
    pieces, uk = refs[:n_pieces], refs[n_pieces]
    pre_out, hid, hid_t, x_out, xs, sem, out_sem = refs[-7:]
    finish = collect(table, pieces, xs, sem, x_out, 256 * half, out_sem)
    pre = jnp.dot(xs[...], uk[...], preferred_element_type=f32)
    pre_out[...] = pre
    h = pre * (0.5 + 0.5 * jnp.tanh(pre * (C + C * 0.044715 * (pre * pre))))
    hid[...] = h.astype(bf16)
    hid_t[...] = h.T.astype(bf16)
    finish()


def hidden_of(half, table, pieces, up_kept, ready, earlier=()):
    n, tile = len(pieces), 256
    across = pl.BlockSpec((256, tile), lambda i: (half, i))
    return pl.pallas_call(
        functools.partial(hidden_kernel, table, n, half),
        grid=(F // tile,),
        in_specs=[ANY] * n
        + [pl.BlockSpec((D, tile), lambda i: (0, i)), ANY]
        + [ANY] * len(earlier),
        out_specs=[across, across, pl.BlockSpec((tile, 256), lambda i: (i, half)), ANY],
        out_shape=[
            jax.ShapeDtypeStruct((512, F), f32),
            jax.ShapeDtypeStruct((512, F), bf16),
            jax.ShapeDtypeStruct((F, 512), bf16),
            jax.ShapeDtypeStruct((512, D), bf16),
        ],
        input_output_aliases={n + 2 + k: k for k in range(len(earlier))},
        scratch_shapes=[
            pltpu.VMEM((256, D), bf16),
            pltpu.SemaphoreType.DMA((len(table),)),
            pltpu.SemaphoreType.DMA,
        ],
        compiler_params=pltpu.CompilerParams(vmem_limit_bytes=VMEM),
        cost_estimate=cost(2 * 256 * D * F, 14 * MIB),
        name="hidden",
    )(*pieces, up_kept, ready, *earlier)


def back_kernel(table, n_pieces, *refs):
    pieces, (dk, pre_ref) = refs[:n_pieces], refs[n_pieces : n_pieces + 2]
    gp, gp_t, d_out, ds, sem, out_sem = refs[-6:]
    finish = collect(table, pieces, ds, sem, d_out, 0, out_sem)
    back = lax.dot_general(ds[...], dk[...], (((1,), (1,)), ((), ())), preferred_element_type=f32)
    pre = pre_ref[...]
    square = pre * pre
    s = 0.5 + 0.5 * jnp.tanh(pre * (C + C * 0.044715 * square))
    g = back * (s + pre * s * (1.0 - s) * (2.0 * C + 6.0 * C * 0.044715 * square))
    gp[...] = g.astype(bf16)
    gp_t[...] = g.T.astype(bf16)
    finish()


def grad_pre_of(pieces, down_kept, pre, ready):
    n, tile = len(pieces), 256
    return pl.pallas_call(
        functools.partial(back_kernel, COTANGENTS, n),
        grid=(F // tile,),
        in_specs=[ANY] * n
        + [
            pl.BlockSpec((tile, D), lambda i: (i, 0)),
            pl.BlockSpec((512, tile), lambda i: (0, i)),
            ANY,
        ],
        out_specs=[
            pl.BlockSpec((512, tile), lambda i: (0, i)),
            pl.BlockSpec((tile, 512), lambda i: (i, 0)),
            ANY,
        ],
        out_shape=[
            jax.ShapeDtypeStruct((512, F), bf16),
            jax.ShapeDtypeStruct((F, 512), bf16),
            jax.ShapeDtypeStruct((512, D), bf16),
        ],
        scratch_shapes=[
            pltpu.VMEM((512, D), bf16),
            pltpu.SemaphoreType.DMA((len(COTANGENTS),)),
            pltpu.SemaphoreType.DMA,
        ],
        compiler_params=pltpu.CompilerParams(vmem_limit_bytes=VMEM),
        cost_estimate=cost(2 * 512 * D * F, 20 * MIB),
        name="grad_pre",
    )(*pieces, down_kept, pre, ready)


def share_kernel(turned, cuts, left, w, _, *outs):
    dims = (((1,), (1 if turned else 0,)), ((), ()))
    total = lax.dot_general(left[...], w[...], dims, preferred_element_type=f32).astype(bf16)
    row = 0
    for out, rows in zip(outs, cuts):
        out[...] = total[row : row + rows, :]
        row += rows


def share(turned, left, block, cuts, w, ready):
    m, tile = sum(cuts), 1024
    return pl.pallas_call(
        functools.partial(share_kernel, turned, cuts),
        grid=(D // tile,),
        in_specs=[
            pl.BlockSpec((m, F), lambda i: (block, 0)),
            pl.BlockSpec((tile, F), lambda i: (i, 0)) if turned else pl.BlockSpec((F, tile), lambda i: (0, i)),
            ANY,
        ],
        out_specs=[pl.BlockSpec((rows, tile), lambda i: (0, i)) for rows in cuts],
        out_shape=[jax.ShapeDtypeStruct((rows, D), bf16) for rows in cuts],
        compiler_params=pltpu.CompilerParams(vmem_limit_bytes=VMEM),
        cost_estimate=cost(2 * m * D * F, 12 * MIB),
        name="share",
    )(left, w, ready)


def packed_kernel(cuts, added, groups, table, left, right, got, _, *refs):
    outs, (a, b, t, buf, add_buf, a_sem, b_sem, got_sem, out_sem) = refs[: len(cuts)], refs[len(cuts) :]
    first = pltpu.make_async_copy(left, a, a_sem)
    first.start()
    rights = []
    for q in range(8):
        col = pl.multiple_of(groups[q] * 256, 256)
        rights.append(pltpu.make_async_copy(right.at[:, pl.ds(col, 256)], b.at[q], b_sem.at[q]))
        rights[q].start()
    if added:
        more = pltpu.make_async_copy(got, add_buf, got_sem)
        more.start()
    places = [(out, k) for out, n in zip(outs, cuts) for k in range(n)]
    moves = [
        pltpu.make_async_copy(buf.at[q], out.at[k], out_sem.at[q]) for q, (out, k) in enumerate(places)
    ]
    first.wait()
    for q in range(8):
        j = groups[q]
        rights[q].wait()
        base = (q % 2) * 4 * F
        for r in range(0, F, 256):
            acc = jnp.dot(a[r : r + 256, :], b[q], preferred_element_type=f32)
            for ct in range(2):
                part = acc[:, ct * 128 : (ct + 1) * 128]
                row = base + ct * F + r
                t[row : row + 256, :] = part.astype(bf16)
                row += 2 * F
                t[row : row + 256, :] = pltpu.roll(part, 64, 1).astype(bf16)
        for p in range(KEPT // 2):
            ra = pl.multiple_of(base + table[j, 2 * p], B)
            rb = pl.multiple_of(base + table[j, 2 * p + 1], B)
            to = slice(p * B, (p + 1) * B)
            buf[q, to, 0:B] = t[pl.ds(ra, B), 0:B]
            buf[q, to, B : 2 * B] = t[pl.ds(rb, B), B : 2 * B]
        if added:
            if q == 0:
                more.wait()
            buf[q] = (buf[q].astype(f32) + add_buf[q].astype(f32)).astype(bf16)
        moves[q].start()
    for move in moves:
        move.wait()


def packed(groups, table, left, right, ready, cuts=(8,), got=None):
    added = got is not None
    return pl.pallas_call(
        functools.partial(packed_kernel, cuts, added),
        grid_spec=pltpu.PrefetchScalarGridSpec(
            num_scalar_prefetch=2,
            grid=(1,),
            in_specs=[ANY] * 4,
            out_specs=[ANY] * len(cuts),
            scratch_shapes=[
                pltpu.VMEM((F, 512), bf16),
                pltpu.VMEM((8, 512, 256), bf16),
                pltpu.VMEM((8 * F, 128), bf16),
                pltpu.VMEM((8, SLAB, 128), bf16),
                pltpu.VMEM((8, SLAB, 128), bf16),
                pltpu.SemaphoreType.DMA,
                pltpu.SemaphoreType.DMA((8,)),
                pltpu.SemaphoreType.DMA,
                pltpu.SemaphoreType.DMA((8,)),
            ],
        ),
        out_shape=[jax.ShapeDtypeStruct((n, SLAB, 128), bf16) for n in cuts],
        compiler_params=pltpu.CompilerParams(vmem_limit_bytes=VMEM),
        cost_estimate=cost(2 * 512 * F * 2048, 6 * MIB),
        name="packed",
    )(groups, table, left, right, got if added else right, ready)


def expand_kernel(turned, keep, table, w, f, out, s, dense):
    total = w[0].astype(f32) + f[0].astype(f32)
    s[0:SLAB, :] = total
    s[SLAB : 2 * SLAB, :] = pltpu.roll(total, 64, 1)
    target = dense if turned else out
    for r in range(16):
        rows = slice(r * B, (r + 1) * B)
        for c in range(4):
            row = pl.multiple_of(table[r * 4 + c], B)
            half = slice((c % 2) * B, (c % 2 + 1) * B)
            block = s[pl.ds(row, B), half]
            target[rows, c * B : (c + 1) * B] = jnp.where(keep[r * 4 + c] != 0, block, 0.0)
    if turned:
        for r in range(0, F, 128):
            for c in range(0, 256, 128):
                out[c : c + 128, r : r + 128] = dense[r : r + 128, c : c + 128].T


def expand(turned, keep, table, w, f):
    slab = pl.BlockSpec((1, SLAB, 128), lambda i, k, p: (0, 0, 0))
    shape = (256, F) if turned else (F, 256)
    return pl.pallas_call(
        functools.partial(expand_kernel, turned),
        grid_spec=pltpu.PrefetchScalarGridSpec(
            num_scalar_prefetch=2,
            grid=(1,),
            in_specs=[slab, slab],
            out_specs=pl.BlockSpec(shape, lambda i, k, p: (0, 0)),
            scratch_shapes=[pltpu.VMEM((2 * SLAB, 128), f32), pltpu.VMEM((F, 256), f32)],
        ),
        out_shape=jax.ShapeDtypeStruct(shape, f32),
        compiler_params=pltpu.CompilerParams(vmem_limit_bytes=VMEM),
        cost_estimate=cost(0, 2 * MIB),
        name="expand",
    )(keep, table, w, f)


def plan(mask_up, mask_down):
    up = mask_up.reshape(16, 4, 16).transpose(0, 2, 1).reshape(16, 64)
    down = mask_down.reshape(16, 16, 4).transpose(1, 0, 2).reshape(16, 64)
    keep = (jnp.stack([up, down]) != 0).astype(jnp.int32)
    place = jnp.arange(64, dtype=jnp.int32)
    slot = jnp.sum(keep[:, :, None, :] * (place[None, :] < place[:, None]), axis=-1)
    wanted = jnp.arange(KEPT, dtype=jnp.int32)
    hit = (slot[:, :, None, :] == wanted[:, None]) & (keep[:, :, None, :] != 0)
    here = (place // 4) * B + ((place % 4) // 2) * F
    turned = (place % 2) ^ (wanted[:, None] % 2)
    source = jnp.sum(jnp.where(hit, here + turned * (2 * F), 0), axis=-1)
    back = (slot // 2) * B + ((slot % 2) ^ (place % 2)) * SLAB
    return source, jnp.where(keep != 0, back, 0), keep


def add(*terms):
    total = terms[0].astype(f32)
    for term in terms[1:]:
        total = total + term.astype(f32)
    return total.astype(bf16)


def cat(*parts):
    return jnp.concatenate(parts, axis=0)


def stage(*values):
    return lax.optimization_barrier(values)


def local(tokens, w_up, w_down, mask_up, mask_down, cotangent):
    x, d = tokens, cotangent
    dp = lax.axis_index("dp")
    y, xh, c = dp // 4, (dp // 2) % 2, dp % 2

    xm, xp = shift(x, dz=1), shift(x, dz=-1)
    l1, r1 = shift(cat(x[:32], d[:32]), dx=1), shift(cat(x[32:], d[32:]), dx=-1)
    uk = kept_weight(w_up, mask_up)
    table, back, keep = plan(mask_up, mask_down)
    own = [lax.dynamic_index_in_dim(v, dp, 1, keepdims=False) for v in (keep, back)]

    xm, xp, l1, r1, uk, table = stage(xm, xp, l1, r1, uk, table)
    ea, eb = shift(cat(xm[:32], d), dz=1), shift(cat(xp[32:], d), dz=-1)
    l2, r2 = shift(cat(xm[:32], xp[:32]), dx=1), shift(cat(xm[32:], xp[32:]), dx=-1)
    dk = kept_weight(w_down, mask_down, xm)

    ea, eb, l2, r2, dk = stage(ea, eb, l2, r2, dk)
    l3 = shift(cat(ea[:32], ea[32:64], eb[32:64]), dx=1)
    r3 = shift(cat(eb[:32], ea[64:], eb[64:]), dx=-1)
    fa, fb = shift(ea[32:64], dz=1), shift(eb[64:], dz=-1)
    half = hidden_of(0, TOKENS_COLUMN, [x, xm, xp, ea, eb], uk, l2)
    (o_col,) = share(False, half[1], 0, (256,), dk, half[1])

    fa, fb, l3, r3, o_col = stage(fa, fb, l3, r3, o_col)
    l4, r4 = shift(fa, dx=1), shift(fb, dx=-1)
    pre, hid, hid_t, xs = hidden_of(1, TOKENS_SIDE, [l1, l2, l3, r1, r2, r3], uk, o_col, half)
    o_left, o_right = share(False, hid, 1, (128, 128), dk, xs)

    oa, ob = shift(o_left, dx=-1), shift(o_right, dx=1)
    gp, gp_t, ds = grad_pre_of([d, ea, eb, fa, fb, l1, l3, l4, r1, r3, r4], dk, pre, o_left)

    def order(pairs):
        return jnp.stack([4 * at + (xh ^ e) * 2 + c for at, e in pairs]).astype(jnp.int32)

    pair, mirror = y ^ 1, 3 - y
    up_order = order(
        [(3 - pair, 0), (pair, 0), (mirror ^ 1, 1), (mirror, 1), (mirror, 0), (y, 0), (pair, 1), (y, 1)]
    )
    down_order = order([(at, e) for at in (3 - pair, pair, mirror, y) for e in (0, 1)])

    (up_away,) = packed(up_order ^ 1, table[0], gp_t, xs, gp)
    up_got = to_core(up_away)
    t_col, t_left, t_right = share(True, gp, 0, (256, 128, 128), uk, up_away)
    ta, tb = shift(t_left, dx=-1), shift(t_right, dx=1)

    def opposite(col, a, b):
        return add(col[192:224], a[96:]), add(col[224:256], b[96:])

    def beside(col, a, b, za, zb):
        p = cat(add(col[128:160], a[64:96], za), add(col[160:192], b[64:96]))
        m = cat(add(col[64:96], a[32:64]), add(col[96:128], b[32:64], zb))
        return p, m

    oa, ob, t_col = stage(oa, ob, t_col)
    o_za, o_zb = stage(*opposite(o_col, oa, ob))
    za, zb = shift(o_za, dz=1), shift(o_zb, dz=-1)
    ua, ub, uc, ud = packed(up_order, table[0], gp_t, xs, o_zb, (2, 2, 2, 2), up_got)
    u1, u2 = to_pair(ua), to_mirror(ub)

    za, zb, uc, ud = stage(za, zb, uc, ud)
    o_p, o_m = stage(*beside(o_col, oa, ob, za, zb))
    o_p_in, o_m_in = shift(o_p, dz=1), shift(o_m, dz=-1)
    (down_away,) = packed(down_order ^ 1, table[1], hid_t, ds, o_m)
    down_got = to_core(down_away)

    u1, u2, uc, ud, ready = stage(u1, u2, uc, ud, down_away)
    u3, u4 = stage(add(uc[0:1], u1[0:1]), add(ud[0:1], u2[0:1]))
    down_send, down_keep = packed(down_order, table[1], hid_t, ds, u4, (4, 4), down_got)
    u3, u4 = to_mirror(u3), to_pair(u4)
    v1 = to_pair(down_send)

    ta, tb, o_p_in, o_m_in, down_keep = stage(ta, tb, o_p_in, o_m_in, down_keep)
    za, zb = opposite(t_col, ta, tb)
    za, zb = shift(za, dz=1), shift(zb, dz=-1)
    output = add(o_col[:64], cat(oa[:32], ob[:32]), o_p_in, o_m_in)

    u3, u4, za, zb, output = stage(u3, u4, za, zb, output)
    t_p, t_m = beside(t_col, ta, tb, za, zb)
    t_p, t_m = shift(t_p, dz=1), shift(t_m, dz=-1)
    up_far = shift(add(ud[1:2], u2[1:2], u4), dx=2)
    up_near = add(uc[1:2], u1[1:2], u3)

    v1, up_near = stage(v1, up_near)
    v2 = to_mirror(add(down_keep[0:2], v1[0:2]))
    grad_up = expand(True, own[0][0], own[1][0], up_near, up_far)

    v2, t_p, t_m, grad_up = stage(v2, t_p, t_m, grad_up)
    down_far = shift(add(down_keep[3:4], v1[3:4], v2[1:2]), dx=2)
    down_near = add(down_keep[2:3], v1[2:3], v2[0:1])
    grad_tokens = add(t_col[:64], cat(ta[:32], tb[:32]), t_p, t_m)
    grad_down = expand(False, own[0][1], own[1][1], down_near, down_far)
    return output, grad_tokens, grad_up, grad_down


def solution(mesh):
    placed = (
        P(("dp", "tensor"), None),
        P(None, "tensor"),
        P("tensor", None),
        P(None, "tensor"),
        P("tensor", None),
        P(("dp", "tensor"), None),
    )
    return jax.shard_map(
        local,
        mesh=mesh,
        in_specs=placed,
        out_specs=(
            P(("dp", "tensor"), None),
            P(("dp", "tensor"), None),
            P("dp", "tensor"),
            P("tensor", "dp"),
        ),
        check_vma=False,
    )
```

```python
import functools
import math

import jax
import jax.numpy as jnp
from jax import lax
from jax.experimental import pallas as pl
from jax.experimental.pallas import tpu as pltpu
from jax.sharding import PartitionSpec as P

B = 64
D = 4096
F = 1024
KEPT = 40
SLAB = KEPT // 2 * B
MIB = 1 << 20
VMEM = 60 * MIB
C = math.sqrt(2.0 / math.pi)
f32, bf16 = jnp.float32, jnp.bfloat16
AXES = ("dp", "tensor")


def device_at(x, y, z, c):
    x, y, z = x % 4, y % 4, z % 4
    return ((y * 2 + x // 2) * 2 + c) * 8 + z * 2 + x % 2


def send(value, to):
    pairs = [
        (device_at(x, y, z, c), device_at(*to(x, y, z, c)))
        for x in range(4)
        for y in range(4)
        for z in range(4)
        for c in range(2)
    ]
    return lax.ppermute(value, AXES, pairs)


def shift(value, dx=0, dz=0):
    return send(value, lambda x, y, z, c: (x + dx, y, z + dz, c))


def to_core(value):
    return send(value, lambda x, y, z, c: (x, y, z, 1 - c))


def to_pair(value):
    return send(value, lambda x, y, z, c: (x, y ^ 1, z, c))


def to_mirror(value):
    return send(value, lambda x, y, z, c: (x, 3 - y, z, c))


def cost(flops, nbytes):
    return pl.CostEstimate(flops=int(flops) * 64, bytes_accessed=int(nbytes) * 64, transcendentals=0)


def spread(blocks):
    row = lax.broadcasted_iota(jnp.int32, (blocks, blocks * B), 0)
    col = lax.broadcasted_iota(jnp.int32, (blocks, blocks * B), 1)
    return (row == col // B).astype(f32).astype(bf16)


def mask_kernel(blocks, per, mask, w, *rest):
    kept, rows = rest[-2:]
    i = pl.program_id(0)

    @pl.when(i == 0)
    def _():
        rows[...] = jnp.dot(
            mask[...].astype(f32).astype(bf16), spread(blocks), preferred_element_type=f32
        )

    for k in range(per):
        at = slice(k * B, (k + 1) * B)
        kept[at, :] = (w[at, :].astype(f32) * rows[pl.ds(per * i + k, 1), :]).astype(bf16)


def kept_weight(w, mask, *ready):
    rows, cols = w.shape
    steps = 4
    block = pl.BlockSpec((rows // steps, cols), lambda i: (i, 0))
    return pl.pallas_call(
        functools.partial(mask_kernel, cols // B, rows // B // steps),
        grid=(steps,),
        in_specs=[pl.BlockSpec(mask.shape, lambda i: (0, 0)), block]
        + [pl.BlockSpec(memory_space=pl.ANY)] * len(ready),
        out_specs=block,
        out_shape=jax.ShapeDtypeStruct((rows, cols), bf16),
        scratch_shapes=[pltpu.VMEM((rows // B, cols), f32)],
        compiler_params=pltpu.CompilerParams(vmem_limit_bytes=VMEM),
        cost_estimate=cost(0, 18 * MIB),
        name="kept_weight",
    )(mask, w, *ready)


TOKENS_COLUMN = ((0, 0, 64, 0), (1, 0, 64, 64), (2, 0, 64, 128), (3, 0, 32, 192), (4, 0, 32, 224))
TOKENS_SIDE = tuple(
    (3 * s + p, 0, n, 128 * s + dst) for s in range(2) for p, n, dst in ((0, 32, 0), (1, 64, 32), (2, 32, 96))
)
COTANGENTS = (
    (0, 0, 64, 0),
    (1, 32, 64, 64),
    (2, 32, 64, 128),
    (3, 0, 32, 192),
    (4, 0, 32, 224),
    (5, 32, 32, 256),
    (6, 32, 64, 288),
    (7, 0, 32, 352),
    (8, 32, 32, 384),
    (9, 32, 64, 416),
    (10, 0, 32, 480),
)
ANY = pl.BlockSpec(memory_space=pl.ANY)


def collect(table, pieces, rows, sem, out, row, out_sem):
    i = pl.program_id(0)
    keep = pltpu.make_async_copy(rows, out.at[pl.ds(row, rows.shape[0]), :], out_sem)

    @pl.when(i == 0)
    def _():
        moves = [
            pltpu.make_async_copy(pieces[p].at[pl.ds(src, n), :], rows.at[pl.ds(dst, n), :], sem.at[k])
            for k, (p, src, n, dst) in enumerate(table)
        ]
        for move in moves:
            move.start()
        for move in moves:
            move.wait()
        keep.start()

    def finish():
        @pl.when(i == pl.num_programs(0) - 1)
        def _():
            keep.wait()

    return finish


def hidden_kernel(table, n_pieces, half, *refs):
    pieces, uk = refs[:n_pieces], refs[n_pieces]
    pre_out, hid, hid_t, x_out, xs, sem, out_sem = refs[-7:]
    finish = collect(table, pieces, xs, sem, x_out, 256 * half, out_sem)
    pre = jnp.dot(xs[...], uk[...], preferred_element_type=f32)
    pre_out[...] = pre
    h = pre * (0.5 + 0.5 * jnp.tanh(pre * (C + C * 0.044715 * (pre * pre))))
    hid[...] = h.astype(bf16)
    hid_t[...] = h.T.astype(bf16)
    finish()


def hidden_of(half, table, pieces, up_kept, ready, earlier=()):
    n, tile = len(pieces), 256
    across = pl.BlockSpec((256, tile), lambda i: (half, i))
    return pl.pallas_call(
        functools.partial(hidden_kernel, table, n, half),
        grid=(F // tile,),
        in_specs=[ANY] * n
        + [pl.BlockSpec((D, tile), lambda i: (0, i)), ANY]
        + [ANY] * len(earlier),
        out_specs=[across, across, pl.BlockSpec((tile, 256), lambda i: (i, half)), ANY],
        out_shape=[
            jax.ShapeDtypeStruct((512, F), f32),
            jax.ShapeDtypeStruct((512, F), bf16),
            jax.ShapeDtypeStruct((F, 512), bf16),
            jax.ShapeDtypeStruct((512, D), bf16),
        ],
        input_output_aliases={n + 2 + k: k for k in range(len(earlier))},
        scratch_shapes=[
            pltpu.VMEM((256, D), bf16),
            pltpu.SemaphoreType.DMA((len(table),)),
            pltpu.SemaphoreType.DMA,
        ],
        compiler_params=pltpu.CompilerParams(vmem_limit_bytes=VMEM),
        cost_estimate=cost(2 * 256 * D * F, 14 * MIB),
        name="hidden",
    )(*pieces, up_kept, ready, *earlier)


def back_kernel(table, n_pieces, *refs):
    pieces, (dk, pre_ref) = refs[:n_pieces], refs[n_pieces : n_pieces + 2]
    gp, gp_t, d_out, ds, sem, out_sem = refs[-6:]
    finish = collect(table, pieces, ds, sem, d_out, 0, out_sem)
    back = lax.dot_general(ds[...], dk[...], (((1,), (1,)), ((), ())), preferred_element_type=f32)
    pre = pre_ref[...]
    square = pre * pre
    s = 0.5 + 0.5 * jnp.tanh(pre * (C + C * 0.044715 * square))
    g = back * (s + pre * s * (1.0 - s) * (2.0 * C + 6.0 * C * 0.044715 * square))
    gp[...] = g.astype(bf16)
    gp_t[...] = g.T.astype(bf16)
    finish()


def grad_pre_of(pieces, down_kept, pre, ready):
    n, tile = len(pieces), 256
    return pl.pallas_call(
        functools.partial(back_kernel, COTANGENTS, n),
        grid=(F // tile,),
        in_specs=[ANY] * n
        + [
            pl.BlockSpec((tile, D), lambda i: (i, 0)),
            pl.BlockSpec((512, tile), lambda i: (0, i)),
            ANY,
        ],
        out_specs=[
            pl.BlockSpec((512, tile), lambda i: (0, i)),
            pl.BlockSpec((tile, 512), lambda i: (i, 0)),
            ANY,
        ],
        out_shape=[
            jax.ShapeDtypeStruct((512, F), bf16),
            jax.ShapeDtypeStruct((F, 512), bf16),
            jax.ShapeDtypeStruct((512, D), bf16),
        ],
        scratch_shapes=[
            pltpu.VMEM((512, D), bf16),
            pltpu.SemaphoreType.DMA((len(COTANGENTS),)),
            pltpu.SemaphoreType.DMA,
        ],
        compiler_params=pltpu.CompilerParams(vmem_limit_bytes=VMEM),
        cost_estimate=cost(2 * 512 * D * F, 20 * MIB),
        name="grad_pre",
    )(*pieces, down_kept, pre, ready)


def share_kernel(turned, cuts, left, w, _, *outs):
    dims = (((1,), (1 if turned else 0,)), ((), ()))
    total = lax.dot_general(left[...], w[...], dims, preferred_element_type=f32).astype(bf16)
    row = 0
    for out, rows in zip(outs, cuts):
        out[...] = total[row : row + rows, :]
        row += rows


def share(turned, left, block, cuts, w, ready):
    m, tile = sum(cuts), 1024
    return pl.pallas_call(
        functools.partial(share_kernel, turned, cuts),
        grid=(D // tile,),
        in_specs=[
            pl.BlockSpec((m, F), lambda i: (block, 0)),
            pl.BlockSpec((tile, F), lambda i: (i, 0)) if turned else pl.BlockSpec((F, tile), lambda i: (0, i)),
            ANY,
        ],
        out_specs=[pl.BlockSpec((rows, tile), lambda i: (0, i)) for rows in cuts],
        out_shape=[jax.ShapeDtypeStruct((rows, D), bf16) for rows in cuts],
        compiler_params=pltpu.CompilerParams(vmem_limit_bytes=VMEM),
        cost_estimate=cost(2 * m * D * F, 12 * MIB),
        name="share",
    )(left, w, ready)


def packed_kernel(cuts, added, groups, table, left, right, got, _, *refs):
    outs, (a, b, t, buf, add_buf, a_sem, b_sem, got_sem, out_sem) = refs[: len(cuts)], refs[len(cuts) :]
    first = pltpu.make_async_copy(left, a, a_sem)
    first.start()
    rights = []
    for q in range(8):
        col = pl.multiple_of(groups[q] * 256, 256)
        rights.append(pltpu.make_async_copy(right.at[:, pl.ds(col, 256)], b.at[q], b_sem.at[q]))
        rights[q].start()
    if added:
        more = pltpu.make_async_copy(got, add_buf, got_sem)
        more.start()
    places = [(out, k) for out, n in zip(outs, cuts) for k in range(n)]
    moves = [
        pltpu.make_async_copy(buf.at[q], out.at[k], out_sem.at[q]) for q, (out, k) in enumerate(places)
    ]
    first.wait()
    for q in range(8):
        j = groups[q]
        rights[q].wait()
        base = (q % 2) * 4 * F
        for r in range(0, F, 256):
            acc = jnp.dot(a[r : r + 256, :], b[q], preferred_element_type=f32)
            for ct in range(2):
                part = acc[:, ct * 128 : (ct + 1) * 128]
                row = base + ct * F + r
                t[row : row + 256, :] = part.astype(bf16)
                row += 2 * F
                t[row : row + 256, :] = pltpu.roll(part, 64, 1).astype(bf16)
        for p in range(KEPT // 2):
            ra = pl.multiple_of(base + table[j, 2 * p], B)
            rb = pl.multiple_of(base + table[j, 2 * p + 1], B)
            to = slice(p * B, (p + 1) * B)
            buf[q, to, 0:B] = t[pl.ds(ra, B), 0:B]
            buf[q, to, B : 2 * B] = t[pl.ds(rb, B), B : 2 * B]
        if added:
            if q == 0:
                more.wait()
            buf[q] = (buf[q].astype(f32) + add_buf[q].astype(f32)).astype(bf16)
        moves[q].start()
    for move in moves:
        move.wait()


def packed(groups, table, left, right, ready, cuts=(8,), got=None):
    added = got is not None
    return pl.pallas_call(
        functools.partial(packed_kernel, cuts, added),
        grid_spec=pltpu.PrefetchScalarGridSpec(
            num_scalar_prefetch=2,
            grid=(1,),
            in_specs=[ANY] * 4,
            out_specs=[ANY] * len(cuts),
            scratch_shapes=[
                pltpu.VMEM((F, 512), bf16),
                pltpu.VMEM((8, 512, 256), bf16),
                pltpu.VMEM((8 * F, 128), bf16),
                pltpu.VMEM((8, SLAB, 128), bf16),
                pltpu.VMEM((8, SLAB, 128), bf16),
                pltpu.SemaphoreType.DMA,
                pltpu.SemaphoreType.DMA((8,)),
                pltpu.SemaphoreType.DMA,
                pltpu.SemaphoreType.DMA((8,)),
            ],
        ),
        out_shape=[jax.ShapeDtypeStruct((n, SLAB, 128), bf16) for n in cuts],
        compiler_params=pltpu.CompilerParams(vmem_limit_bytes=VMEM),
        cost_estimate=cost(2 * 512 * F * 2048, 6 * MIB),
        name="packed",
    )(groups, table, left, right, got if added else right, ready)


def expand_kernel(turned, keep, table, w, f, out, s, dense):
    total = w[0].astype(f32) + f[0].astype(f32)
    s[0:SLAB, :] = total
    s[SLAB : 2 * SLAB, :] = pltpu.roll(total, 64, 1)
    target = dense if turned else out
    for r in range(16):
        rows = slice(r * B, (r + 1) * B)
        for c in range(4):
            row = pl.multiple_of(table[r * 4 + c], B)
            half = slice((c % 2) * B, (c % 2 + 1) * B)
            block = s[pl.ds(row, B), half]
            target[rows, c * B : (c + 1) * B] = jnp.where(keep[r * 4 + c] != 0, block, 0.0)
    if turned:
        for r in range(0, F, 128):
            for c in range(0, 256, 128):
                out[c : c + 128, r : r + 128] = dense[r : r + 128, c : c + 128].T


def expand(turned, keep, table, w, f):
    slab = pl.BlockSpec((1, SLAB, 128), lambda i, k, p: (0, 0, 0))
    shape = (256, F) if turned else (F, 256)
    return pl.pallas_call(
        functools.partial(expand_kernel, turned),
        grid_spec=pltpu.PrefetchScalarGridSpec(
            num_scalar_prefetch=2,
            grid=(1,),
            in_specs=[slab, slab],
            out_specs=pl.BlockSpec(shape, lambda i, k, p: (0, 0)),
            scratch_shapes=[pltpu.VMEM((2 * SLAB, 128), f32), pltpu.VMEM((F, 256), f32)],
        ),
        out_shape=jax.ShapeDtypeStruct(shape, f32),
        compiler_params=pltpu.CompilerParams(vmem_limit_bytes=VMEM),
        cost_estimate=cost(0, 2 * MIB),
        name="expand",
    )(keep, table, w, f)


def plan(mask_up, mask_down):
    up = mask_up.reshape(16, 4, 16).transpose(0, 2, 1).reshape(16, 64)
    down = mask_down.reshape(16, 16, 4).transpose(1, 0, 2).reshape(16, 64)
    keep = (jnp.stack([up, down]) != 0).astype(jnp.int32)
    place = jnp.arange(64, dtype=jnp.int32)
    slot = jnp.sum(keep[:, :, None, :] * (place[None, :] < place[:, None]), axis=-1)
    wanted = jnp.arange(KEPT, dtype=jnp.int32)
    hit = (slot[:, :, None, :] == wanted[:, None]) & (keep[:, :, None, :] != 0)
    here = (place // 4) * B + ((place % 4) // 2) * F
    turned = (place % 2) ^ (wanted[:, None] % 2)
    source = jnp.sum(jnp.where(hit, here + turned * (2 * F), 0), axis=-1)
    back = (slot // 2) * B + ((slot % 2) ^ (place % 2)) * SLAB
    return source, jnp.where(keep != 0, back, 0), keep


def add(*terms):
    total = terms[0].astype(f32)
    for term in terms[1:]:
        total = total + term.astype(f32)
    return total.astype(bf16)


def cat(*parts):
    return jnp.concatenate(parts, axis=0)


def stage(*values):
    return lax.optimization_barrier(values)


def local(tokens, w_up, w_down, mask_up, mask_down, cotangent):
    x, d = tokens, cotangent
    dp = lax.axis_index("dp")
    y, xh, c = dp // 4, (dp // 2) % 2, dp % 2

    xm, xp = shift(x, dz=1), shift(x, dz=-1)
    l1, r1 = shift(cat(x[:32], d[:32]), dx=1), shift(cat(x[32:], d[32:]), dx=-1)
    uk = kept_weight(w_up, mask_up)
    table, back, keep = plan(mask_up, mask_down)
    own = [lax.dynamic_index_in_dim(v, dp, 1, keepdims=False) for v in (keep, back)]

    xm, xp, l1, r1, uk, table = stage(xm, xp, l1, r1, uk, table)
    ea, eb = shift(cat(xm[:32], d), dz=1), shift(cat(xp[32:], d), dz=-1)
    l2, r2 = shift(cat(xm[:32], xp[:32]), dx=1), shift(cat(xm[32:], xp[32:]), dx=-1)
    dk = kept_weight(w_down, mask_down, xm)

    ea, eb, l2, r2, dk = stage(ea, eb, l2, r2, dk)
    l3 = shift(cat(ea[:32], ea[32:64], eb[32:64]), dx=1)
    r3 = shift(cat(eb[:32], ea[64:], eb[64:]), dx=-1)
    fa, fb = shift(ea[32:64], dz=1), shift(eb[64:], dz=-1)
    half = hidden_of(0, TOKENS_COLUMN, [x, xm, xp, ea, eb], uk, l2)
    (o_col,) = share(False, half[1], 0, (256,), dk, half[1])

    fa, fb, l3, r3, o_col = stage(fa, fb, l3, r3, o_col)
    l4, r4 = shift(fa, dx=1), shift(fb, dx=-1)
    pre, hid, hid_t, xs = hidden_of(1, TOKENS_SIDE, [l1, l2, l3, r1, r2, r3], uk, o_col, half)
    o_left, o_right = share(False, hid, 1, (128, 128), dk, xs)

    oa, ob = shift(o_left, dx=-1), shift(o_right, dx=1)
    gp, gp_t, ds = grad_pre_of([d, ea, eb, fa, fb, l1, l3, l4, r1, r3, r4], dk, pre, o_left)

    pair, mirror = y ^ 1, 3 - y
    pairs = [(3 - pair, 0), (pair, 0), (mirror ^ 1, 1), (mirror, 1), (mirror, 0), (y, 0), (pair, 1), (y, 1)]
    near = jnp.stack([4 * at + (xh ^ e) * 2 + c for at, e in pairs]).astype(jnp.int32)
    away = near ^ 1
    cuts = (2, 2, 2, 2)

    (up_away,) = packed(away, table[0], gp_t, xs, gp)
    up_got = to_core(up_away)
    t_col, t_left, t_right = share(True, gp, 0, (256, 128, 128), uk, up_away)

    oa, ob, t_col, t_left, t_right = stage(oa, ob, t_col, t_left, t_right)
    ta, tb = shift(t_left, dx=-1), shift(t_right, dx=1)
    ua, ub, uc, ud = packed(near, table[0], gp_t, xs, t_col, cuts, up_got)
    u1, u2 = to_pair(ua), to_mirror(ub)
    (down_away,) = packed(away, table[1], hid_t, ds, ud)
    down_got = to_core(down_away)

    ta, tb, u1, u2, down_away = stage(ta, tb, u1, u2, down_away)
    za, zb = stage(
        cat(add(o_col[192:224], oa[96:]), add(t_col[192:224], ta[96:])),
        cat(add(o_col[224:256], ob[96:]), add(t_col[224:256], tb[96:])),
    )
    da, db, dc, dd = packed(near, table[1], hid_t, ds, zb, cuts, down_got)
    za, zb = shift(za, dz=1), shift(zb, dz=-1)
    d1, d2 = to_pair(da), to_mirror(db)

    dc, dd, u1, u2 = stage(dc, dd, u1, u2)
    u3, u4 = stage(add(uc[0:1], u1[0:1]), add(ud[0:1], u2[0:1]))
    u3, u4 = to_mirror(u3), to_pair(u4)

    za, zb, dc = stage(za, zb, dc)

    def beside(col, a, b, za, zb):
        p = add(col[128:160], a[64:96], za), add(col[160:192], b[64:96])
        m = add(col[64:96], a[32:64]), add(col[96:128], b[32:64], zb)
        return p, m

    o_p, o_m = beside(o_col, oa, ob, za[:32], zb[:32])
    t_p, t_m = beside(t_col, ta, tb, za[32:], zb[32:])
    p, m = stage(cat(*o_p, *t_p), cat(*o_m, *t_m))
    p, m = shift(p, dz=1), shift(m, dz=-1)

    u3, u4, d1, d2 = stage(u3, u4, d1, d2)
    d3, d4 = stage(add(dc[0:1], d1[0:1]), add(dd[0:1], d2[0:1]))
    d3, d4 = to_mirror(d3), to_pair(d4)
    up_far = shift(add(ud[1:2], u2[1:2], u4), dx=2)
    up_near = add(uc[1:2], u1[1:2], u3)
    grad_up = expand(True, own[0][0], own[1][0], up_near, up_far)

    d3, d4, grad_up = stage(d3, d4, grad_up)
    down_far = shift(add(dd[1:2], d2[1:2], d4), dx=2)
    down_near = add(dc[1:2], d1[1:2], d3)
    output = add(o_col[:64], cat(oa[:32], ob[:32]), p[:64], m[:64])
    grad_tokens = add(t_col[:64], cat(ta[:32], tb[:32]), p[64:], m[64:])
    grad_down = expand(False, own[0][1], own[1][1], down_near, down_far)
    return output, grad_tokens, grad_up, grad_down


def solution(mesh):
    placed = (
        P(("dp", "tensor"), None),
        P(None, "tensor"),
        P("tensor", None),
        P(None, "tensor"),
        P("tensor", None),
        P(("dp", "tensor"), None),
    )
    return jax.shard_map(
        local,
        mesh=mesh,
        in_specs=placed,
        out_specs=(
            P(("dp", "tensor"), None),
            P(("dp", "tensor"), None),
            P("dp", "tensor"),
            P("tensor", "dp"),
        ),
        check_vma=False,
    )
```

```python
import functools
import math

import jax
import jax.numpy as jnp
from jax import lax
from jax.experimental import pallas as pl
from jax.experimental.pallas import tpu as pltpu
from jax.sharding import PartitionSpec as P

B = 64
D = 4096
F = 1024
KEPT = 40
SLAB = KEPT // 2 * B
MIB = 1 << 20
VMEM = 60 * MIB
C = math.sqrt(2.0 / math.pi)
f32, bf16 = jnp.float32, jnp.bfloat16
AXES = ("dp", "tensor")


def device_at(x, y, z, c):
    x, y, z = x % 4, y % 4, z % 4
    return ((y * 2 + x // 2) * 2 + c) * 8 + z * 2 + x % 2


def send(value, to):
    pairs = [
        (device_at(x, y, z, c), device_at(*to(x, y, z, c)))
        for x in range(4)
        for y in range(4)
        for z in range(4)
        for c in range(2)
    ]
    return lax.ppermute(value, AXES, pairs)


def shift(value, dx=0, dz=0):
    return send(value, lambda x, y, z, c: (x + dx, y, z + dz, c))


def to_core(value):
    return send(value, lambda x, y, z, c: (x, y, z, 1 - c))


def to_pair(value):
    return send(value, lambda x, y, z, c: (x, y ^ 1, z, c))


def to_mirror(value):
    return send(value, lambda x, y, z, c: (x, 3 - y, z, c))


def cost(flops, nbytes):
    return pl.CostEstimate(flops=int(flops) * 64, bytes_accessed=int(nbytes) * 64, transcendentals=0)


def spread(blocks):
    row = lax.broadcasted_iota(jnp.int32, (blocks, blocks * B), 0)
    col = lax.broadcasted_iota(jnp.int32, (blocks, blocks * B), 1)
    return (row == col // B).astype(f32).astype(bf16)


def mask_kernel(blocks, per, mask, w, *rest):
    kept, rows = rest[-2:]
    i = pl.program_id(0)

    @pl.when(i == 0)
    def _():
        rows[...] = jnp.dot(
            mask[...].astype(f32).astype(bf16), spread(blocks), preferred_element_type=f32
        )

    for k in range(per):
        at = slice(k * B, (k + 1) * B)
        kept[at, :] = (w[at, :].astype(f32) * rows[pl.ds(per * i + k, 1), :]).astype(bf16)


def kept_weight(w, mask, *ready):
    rows, cols = w.shape
    steps = 4
    block = pl.BlockSpec((rows // steps, cols), lambda i: (i, 0))
    return pl.pallas_call(
        functools.partial(mask_kernel, cols // B, rows // B // steps),
        grid=(steps,),
        in_specs=[pl.BlockSpec(mask.shape, lambda i: (0, 0)), block]
        + [pl.BlockSpec(memory_space=pl.ANY)] * len(ready),
        out_specs=block,
        out_shape=jax.ShapeDtypeStruct((rows, cols), bf16),
        scratch_shapes=[pltpu.VMEM((rows // B, cols), f32)],
        compiler_params=pltpu.CompilerParams(vmem_limit_bytes=VMEM),
        cost_estimate=cost(0, 18 * MIB),
        name="kept_weight",
    )(mask, w, *ready)


TOKENS_COLUMN = ((0, 0, 64, 0), (1, 0, 64, 64), (2, 0, 64, 128), (3, 0, 32, 192), (4, 0, 32, 224))
TOKENS_SIDE = tuple(
    (3 * s + p, 0, n, 128 * s + dst) for s in range(2) for p, n, dst in ((0, 32, 0), (1, 64, 32), (2, 32, 96))
)
COTANGENTS = (
    (0, 0, 64, 0),
    (1, 32, 64, 64),
    (2, 32, 64, 128),
    (3, 0, 32, 192),
    (4, 0, 32, 224),
    (5, 32, 32, 256),
    (6, 32, 64, 288),
    (7, 0, 32, 352),
    (8, 32, 32, 384),
    (9, 32, 64, 416),
    (10, 0, 32, 480),
)
ANY = pl.BlockSpec(memory_space=pl.ANY)


def collect(table, pieces, rows, sem, out, row, out_sem):
    i = pl.program_id(0)
    keep = pltpu.make_async_copy(rows, out.at[pl.ds(row, rows.shape[0]), :], out_sem)

    @pl.when(i == 0)
    def _():
        moves = [
            pltpu.make_async_copy(pieces[p].at[pl.ds(src, n), :], rows.at[pl.ds(dst, n), :], sem.at[k])
            for k, (p, src, n, dst) in enumerate(table)
        ]
        for move in moves:
            move.start()
        for move in moves:
            move.wait()
        keep.start()

    def finish():
        @pl.when(i == pl.num_programs(0) - 1)
        def _():
            keep.wait()

    return finish


def hidden_kernel(table, n_pieces, half, *refs):
    pieces, uk = refs[:n_pieces], refs[n_pieces]
    pre_out, hid, hid_t, x_out, xs, sem, out_sem = refs[-7:]
    finish = collect(table, pieces, xs, sem, x_out, 256 * half, out_sem)
    pre = jnp.dot(xs[...], uk[...], preferred_element_type=f32)
    pre_out[...] = pre
    h = pre * (0.5 + 0.5 * jnp.tanh(pre * (C + C * 0.044715 * (pre * pre))))
    hid[...] = h.astype(bf16)
    hid_t[...] = h.T.astype(bf16)
    finish()


def hidden_of(half, table, pieces, up_kept, ready, earlier=()):
    n, tile = len(pieces), 256
    across = pl.BlockSpec((256, tile), lambda i: (half, i))
    return pl.pallas_call(
        functools.partial(hidden_kernel, table, n, half),
        grid=(F // tile,),
        in_specs=[ANY] * n
        + [pl.BlockSpec((D, tile), lambda i: (0, i)), ANY]
        + [ANY] * len(earlier),
        out_specs=[across, across, pl.BlockSpec((tile, 256), lambda i: (i, half)), ANY],
        out_shape=[
            jax.ShapeDtypeStruct((512, F), f32),
            jax.ShapeDtypeStruct((512, F), bf16),
            jax.ShapeDtypeStruct((F, 512), bf16),
            jax.ShapeDtypeStruct((512, D), bf16),
        ],
        input_output_aliases={n + 2 + k: k for k in range(len(earlier))},
        scratch_shapes=[
            pltpu.VMEM((256, D), bf16),
            pltpu.SemaphoreType.DMA((len(table),)),
            pltpu.SemaphoreType.DMA,
        ],
        compiler_params=pltpu.CompilerParams(vmem_limit_bytes=VMEM),
        cost_estimate=cost(2 * 256 * D * F, 14 * MIB),
        name="hidden",
    )(*pieces, up_kept, ready, *earlier)


def back_kernel(table, n_pieces, *refs):
    pieces, (dk, pre_ref) = refs[:n_pieces], refs[n_pieces : n_pieces + 2]
    gp, gp_t, d_out, ds, sem, out_sem = refs[-6:]
    finish = collect(table, pieces, ds, sem, d_out, 0, out_sem)
    back = lax.dot_general(ds[...], dk[...], (((1,), (1,)), ((), ())), preferred_element_type=f32)
    pre = pre_ref[...]
    square = pre * pre
    s = 0.5 + 0.5 * jnp.tanh(pre * (C + C * 0.044715 * square))
    g = back * (s + pre * s * (1.0 - s) * (2.0 * C + 6.0 * C * 0.044715 * square))
    gp[...] = g.astype(bf16)
    gp_t[...] = g.T.astype(bf16)
    finish()


def grad_pre_of(pieces, down_kept, pre, ready):
    n, tile = len(pieces), 256
    return pl.pallas_call(
        functools.partial(back_kernel, COTANGENTS, n),
        grid=(F // tile,),
        in_specs=[ANY] * n
        + [
            pl.BlockSpec((tile, D), lambda i: (i, 0)),
            pl.BlockSpec((512, tile), lambda i: (0, i)),
            ANY,
        ],
        out_specs=[
            pl.BlockSpec((512, tile), lambda i: (0, i)),
            pl.BlockSpec((tile, 512), lambda i: (i, 0)),
            ANY,
        ],
        out_shape=[
            jax.ShapeDtypeStruct((512, F), bf16),
            jax.ShapeDtypeStruct((F, 512), bf16),
            jax.ShapeDtypeStruct((512, D), bf16),
        ],
        scratch_shapes=[
            pltpu.VMEM((512, D), bf16),
            pltpu.SemaphoreType.DMA((len(COTANGENTS),)),
            pltpu.SemaphoreType.DMA,
        ],
        compiler_params=pltpu.CompilerParams(vmem_limit_bytes=VMEM),
        cost_estimate=cost(2 * 512 * D * F, 20 * MIB),
        name="grad_pre",
    )(*pieces, down_kept, pre, ready)


def share_kernel(turned, cuts, left, w, _, *outs):
    dims = (((1,), (1 if turned else 0,)), ((), ()))
    total = lax.dot_general(left[...], w[...], dims, preferred_element_type=f32).astype(bf16)
    row = 0
    for out, rows in zip(outs, cuts):
        out[...] = total[row : row + rows, :]
        row += rows


def share(turned, left, block, cuts, w, ready):
    m, tile = sum(cuts), 1024
    return pl.pallas_call(
        functools.partial(share_kernel, turned, cuts),
        grid=(D // tile,),
        in_specs=[
            pl.BlockSpec((m, F), lambda i: (block, 0)),
            pl.BlockSpec((tile, F), lambda i: (i, 0)) if turned else pl.BlockSpec((F, tile), lambda i: (0, i)),
            ANY,
        ],
        out_specs=[pl.BlockSpec((rows, tile), lambda i: (0, i)) for rows in cuts],
        out_shape=[jax.ShapeDtypeStruct((rows, D), bf16) for rows in cuts],
        compiler_params=pltpu.CompilerParams(vmem_limit_bytes=VMEM),
        cost_estimate=cost(2 * m * D * F, 12 * MIB),
        name="share",
    )(left, w, ready)


def row_sums_kernel(plan, n, *refs):
    for out, segments in zip(refs[n + 1 :], plan):
        for k, terms in enumerate(segments):
            total = refs[terms[0]][...].astype(f32)
            for term in terms[1:]:
                total = total + refs[term][...].astype(f32)
            out[32 * k : 32 * (k + 1), :] = total.astype(bf16)


def row_sums(outs, ready):
    arrays, specs, plan = [], [], []
    tile = D // 2
    for segments in outs:
        plan.append([])
        for terms in segments:
            plan[-1].append(range(len(arrays), len(arrays) + len(terms)))
            for array, row in terms:
                arrays.append(array)
                specs.append(pl.BlockSpec((32, tile), lambda i, at=row // 32: (at, i)))
    return pl.pallas_call(
        functools.partial(row_sums_kernel, plan, len(arrays)),
        grid=(D // tile,),
        in_specs=specs + [ANY],
        out_specs=[pl.BlockSpec((32 * len(segments), tile), lambda i: (0, i)) for segments in outs],
        out_shape=[jax.ShapeDtypeStruct((32 * len(segments), D), bf16) for segments in outs],
        compiler_params=pltpu.CompilerParams(vmem_limit_bytes=VMEM),
        cost_estimate=cost(0, 3 * MIB),
        name="row_sums",
    )(*arrays, ready)


def packed_kernel(cuts, added, groups, table, left, right, got, _, *refs):
    outs, (a, b, t, buf, add_buf, a_sem, b_sem, got_sem, out_sem) = refs[: len(cuts)], refs[len(cuts) :]
    first = pltpu.make_async_copy(left, a, a_sem)
    first.start()
    rights = []
    for q in range(8):
        col = pl.multiple_of(groups[q] * 256, 256)
        rights.append(pltpu.make_async_copy(right.at[:, pl.ds(col, 256)], b.at[q], b_sem.at[q]))
        rights[q].start()
    if added:
        more = pltpu.make_async_copy(got, add_buf, got_sem)
        more.start()
    places = [(out, k) for out, n in zip(outs, cuts) for k in range(n)]
    moves = [
        pltpu.make_async_copy(buf.at[q], out.at[k], out_sem.at[q]) for q, (out, k) in enumerate(places)
    ]
    first.wait()
    for q in range(8):
        j = groups[q]
        rights[q].wait()
        base = (q % 2) * 4 * F
        for r in range(0, F, 256):
            acc = jnp.dot(a[r : r + 256, :], b[q], preferred_element_type=f32)
            for ct in range(2):
                part = acc[:, ct * 128 : (ct + 1) * 128]
                row = base + ct * F + r
                t[row : row + 256, :] = part.astype(bf16)
                row += 2 * F
                t[row : row + 256, :] = pltpu.roll(part, 64, 1).astype(bf16)
        for p in range(KEPT // 2):
            ra = pl.multiple_of(base + table[j, 2 * p], B)
            rb = pl.multiple_of(base + table[j, 2 * p + 1], B)
            to = slice(p * B, (p + 1) * B)
            buf[q, to, 0:B] = t[pl.ds(ra, B), 0:B]
            buf[q, to, B : 2 * B] = t[pl.ds(rb, B), B : 2 * B]
        if added:
            if q == 0:
                more.wait()
            buf[q] = (buf[q].astype(f32) + add_buf[q].astype(f32)).astype(bf16)
        moves[q].start()
    for move in moves:
        move.wait()


def packed(groups, table, left, right, ready, cuts=(8,), got=None):
    added = got is not None
    return pl.pallas_call(
        functools.partial(packed_kernel, cuts, added),
        grid_spec=pltpu.PrefetchScalarGridSpec(
            num_scalar_prefetch=2,
            grid=(1,),
            in_specs=[ANY] * 4,
            out_specs=[ANY] * len(cuts),
            scratch_shapes=[
                pltpu.VMEM((F, 512), bf16),
                pltpu.VMEM((8, 512, 256), bf16),
                pltpu.VMEM((8 * F, 128), bf16),
                pltpu.VMEM((8, SLAB, 128), bf16),
                pltpu.VMEM((8, SLAB, 128), bf16),
                pltpu.SemaphoreType.DMA,
                pltpu.SemaphoreType.DMA((8,)),
                pltpu.SemaphoreType.DMA,
                pltpu.SemaphoreType.DMA((8,)),
            ],
        ),
        out_shape=[jax.ShapeDtypeStruct((n, SLAB, 128), bf16) for n in cuts],
        compiler_params=pltpu.CompilerParams(vmem_limit_bytes=VMEM),
        cost_estimate=cost(2 * 512 * F * 2048, 6 * MIB),
        name="packed",
    )(groups, table, left, right, got if added else right, ready)


def expand_kernel(turned, keep, table, w, f, out, s, dense):
    total = w[0].astype(f32) + f[0].astype(f32)
    s[0:SLAB, :] = total
    s[SLAB : 2 * SLAB, :] = pltpu.roll(total, 64, 1)
    target = dense if turned else out
    for r in range(16):
        rows = slice(r * B, (r + 1) * B)
        for c in range(4):
            row = pl.multiple_of(table[r * 4 + c], B)
            half = slice((c % 2) * B, (c % 2 + 1) * B)
            block = s[pl.ds(row, B), half]
            target[rows, c * B : (c + 1) * B] = jnp.where(keep[r * 4 + c] != 0, block, 0.0)
    if turned:
        for r in range(0, F, 128):
            for c in range(0, 256, 128):
                out[c : c + 128, r : r + 128] = dense[r : r + 128, c : c + 128].T


def expand(turned, keep, table, w, f):
    slab = pl.BlockSpec((1, SLAB, 128), lambda i, k, p: (0, 0, 0))
    shape = (256, F) if turned else (F, 256)
    return pl.pallas_call(
        functools.partial(expand_kernel, turned),
        grid_spec=pltpu.PrefetchScalarGridSpec(
            num_scalar_prefetch=2,
            grid=(1,),
            in_specs=[slab, slab],
            out_specs=pl.BlockSpec(shape, lambda i, k, p: (0, 0)),
            scratch_shapes=[pltpu.VMEM((2 * SLAB, 128), f32), pltpu.VMEM((F, 256), f32)],
        ),
        out_shape=jax.ShapeDtypeStruct(shape, f32),
        compiler_params=pltpu.CompilerParams(vmem_limit_bytes=VMEM),
        cost_estimate=cost(0, 2 * MIB),
        name="expand",
    )(keep, table, w, f)


def plan(mask_up, mask_down):
    up = mask_up.reshape(16, 4, 16).transpose(0, 2, 1).reshape(16, 64)
    down = mask_down.reshape(16, 16, 4).transpose(1, 0, 2).reshape(16, 64)
    keep = (jnp.stack([up, down]) != 0).astype(jnp.int32)
    place = jnp.arange(64, dtype=jnp.int32)
    slot = jnp.sum(keep[:, :, None, :] * (place[None, :] < place[:, None]), axis=-1)
    wanted = jnp.arange(KEPT, dtype=jnp.int32)
    hit = (slot[:, :, None, :] == wanted[:, None]) & (keep[:, :, None, :] != 0)
    here = (place // 4) * B + ((place % 4) // 2) * F
    turned = (place % 2) ^ (wanted[:, None] % 2)
    source = jnp.sum(jnp.where(hit, here + turned * (2 * F), 0), axis=-1)
    back = (slot // 2) * B + ((slot % 2) ^ (place % 2)) * SLAB
    return source, jnp.where(keep != 0, back, 0), keep


def add(*terms):
    total = terms[0].astype(f32)
    for term in terms[1:]:
        total = total + term.astype(f32)
    return total.astype(bf16)


def cat(*parts):
    return jnp.concatenate(parts, axis=0)


def stage(*values):
    return lax.optimization_barrier(values)


def local(tokens, w_up, w_down, mask_up, mask_down, cotangent):
    x, d = tokens, cotangent
    dp = lax.axis_index("dp")
    y, xh, c = dp // 4, (dp // 2) % 2, dp % 2

    xm, xp = shift(x, dz=1), shift(x, dz=-1)
    l1, r1 = shift(cat(x[:32], d[:32]), dx=1), shift(cat(x[32:], d[32:]), dx=-1)
    uk = kept_weight(w_up, mask_up)
    table, back, keep = plan(mask_up, mask_down)
    own = [lax.dynamic_index_in_dim(v, dp, 1, keepdims=False) for v in (keep, back)]

    xm, xp, l1, r1, uk, table = stage(xm, xp, l1, r1, uk, table)
    ea, eb = shift(cat(xm[:32], d), dz=1), shift(cat(xp[32:], d), dz=-1)
    l2, r2 = shift(cat(xm[:32], xp[:32]), dx=1), shift(cat(xm[32:], xp[32:]), dx=-1)
    dk = kept_weight(w_down, mask_down, xm)

    ea, eb, l2, r2, dk = stage(ea, eb, l2, r2, dk)
    l3 = shift(cat(ea[:32], ea[32:64], eb[32:64]), dx=1)
    r3 = shift(cat(eb[:32], ea[64:], eb[64:]), dx=-1)
    fa, fb = shift(ea[32:64], dz=1), shift(eb[64:], dz=-1)
    half = hidden_of(0, TOKENS_COLUMN, [x, xm, xp, ea, eb], uk, l2)
    (o_col,) = share(False, half[1], 0, (256,), dk, half[1])

    fa, fb, l3, r3, o_col = stage(fa, fb, l3, r3, o_col)
    l4, r4 = shift(fa, dx=1), shift(fb, dx=-1)
    pre, hid, hid_t, xs = hidden_of(1, TOKENS_SIDE, [l1, l2, l3, r1, r2, r3], uk, o_col, half)
    o_left, o_right = share(False, hid, 1, (128, 128), dk, xs)

    oa, ob = shift(o_left, dx=-1), shift(o_right, dx=1)
    gp, gp_t, ds = grad_pre_of([d, ea, eb, fa, fb, l1, l3, l4, r1, r3, r4], dk, pre, o_left)

    pair, mirror = y ^ 1, 3 - y
    pairs = [(3 - pair, 0), (pair, 0), (mirror ^ 1, 1), (mirror, 1), (mirror, 0), (y, 0), (pair, 1), (y, 1)]
    near = jnp.stack([4 * at + (xh ^ e) * 2 + c for at, e in pairs]).astype(jnp.int32)
    away = near ^ 1
    cuts = (2, 2, 2, 2)

    (up_away,) = packed(away, table[0], gp_t, xs, gp)
    up_got = to_core(up_away)
    t_col, t_left, t_right = share(True, gp, 0, (256, 128, 128), uk, up_away)

    oa, ob, t_col, t_left, t_right = stage(oa, ob, t_col, t_left, t_right)
    ta, tb = shift(t_left, dx=-1), shift(t_right, dx=1)
    (down_away,) = packed(away, table[1], hid_t, ds, t_col)
    down_got = to_core(down_away)
    ua, ub, uc, ud = packed(near, table[0], gp_t, xs, down_away, cuts, up_got)
    u1, u2 = to_pair(ua), to_mirror(ub)
    da, db, dc, dd = packed(near, table[1], hid_t, ds, ud, cuts, down_got)

    ta, tb, dd = stage(ta, tb, dd)
    o, t, a, b, g, h = o_col, t_col, oa, ob, ta, tb
    za, zb = row_sums(
        [
            [[(o, 192), (a, 96)], [(t, 192), (g, 96)]],
            [[(o, 224), (b, 96)], [(t, 224), (h, 96)]],
        ],
        dd,
    )
    da, db, za, zb = stage(da, db, za, zb)
    za, zb = shift(za, dz=1), shift(zb, dz=-1)
    u1, u2, da, db = stage(u1, u2, da, db)
    d1, d2 = to_pair(da), to_mirror(db)

    p, m = row_sums(
        [
            [[(o, 128), (a, 64), (za, 0)], [(o, 160), (b, 64)], [(t, 128), (g, 64), (za, 32)], [(t, 160), (h, 64)]],
            [[(o, 64), (a, 32)], [(o, 96), (b, 32), (zb, 0)], [(t, 64), (g, 32)], [(t, 96), (h, 32), (zb, 32)]],
        ],
        da,
    )
    u1, u2, p, m = stage(u1, u2, p, m)
    p, m = shift(p, dz=1), shift(m, dz=-1)
    u3, u4 = stage(add(uc[0:1], u1[0:1]), add(ud[0:1], u2[0:1]))
    u3, u4 = to_mirror(u3), to_pair(u4)
    d1, d2, dc, _ = stage(d1, d2, dc, u1)
    d3, d4 = to_mirror(add(dc[0:1], d1[0:1])), to_pair(add(dd[0:1], d2[0:1]))

    u3, u4, dc = stage(u3, u4, dc)
    up_far = shift(add(ud[1:2], u2[1:2], u4), dx=2)
    up_near = add(uc[1:2], u1[1:2], u3)
    grad_up = expand(True, own[0][0], own[1][0], up_near, up_far)

    d3, d4, grad_up = stage(d3, d4, grad_up)
    down_far = shift(add(dd[1:2], d2[1:2], d4), dx=2)
    down_near = add(dc[1:2], d1[1:2], d3)
    output, grad_tokens = row_sums(
        [
            [[(o, 0), (a, 0), (p, 0), (m, 0)], [(o, 32), (b, 0), (p, 32), (m, 32)]],
            [[(t, 0), (g, 0), (p, 64), (m, 64)], [(t, 32), (h, 0), (p, 96), (m, 96)]],
        ],
        down_near,
    )
    grad_down = expand(False, own[0][1], own[1][1], down_near, down_far)
    return output, grad_tokens, grad_up, grad_down


def solution(mesh):
    placed = (
        P(("dp", "tensor"), None),
        P(None, "tensor"),
        P("tensor", None),
        P(None, "tensor"),
        P("tensor", None),
        P(("dp", "tensor"), None),
    )
    return jax.shard_map(
        local,
        mesh=mesh,
        in_specs=placed,
        out_specs=(
            P(("dp", "tensor"), None),
            P(("dp", "tensor"), None),
            P("dp", "tensor"),
            P("tensor", "dp"),
        ),
        check_vma=False,
    )
```

```python
import functools
import math

import jax
import jax.numpy as jnp
from jax import lax
from jax.experimental import pallas as pl
from jax.experimental.pallas import tpu as pltpu
from jax.sharding import PartitionSpec as P

B = 64
D = 4096
F = 1024
KEPT = 40
SLAB = KEPT // 2 * B
MIB = 1 << 20
VMEM = 40 * MIB
C = math.sqrt(2.0 / math.pi)
f32, bf16 = jnp.float32, jnp.bfloat16
AXES = ("dp", "tensor")


def device_at(x, y, z, c):
    x, y, z = x % 4, y % 4, z % 4
    return ((y * 2 + x // 2) * 2 + c) * 8 + z * 2 + x % 2


def send(value, to):
    pairs = [
        (device_at(x, y, z, c), device_at(*to(x, y, z, c)))
        for x in range(4)
        for y in range(4)
        for z in range(4)
        for c in range(2)
    ]
    return lax.ppermute(value, AXES, pairs)


def shift(value, dx=0, dz=0):
    return send(value, lambda x, y, z, c: (x + dx, y, z + dz, c))


def to_core(value):
    return send(value, lambda x, y, z, c: (x, y, z, 1 - c))


def to_pair(value):
    return send(value, lambda x, y, z, c: (x, y ^ 1, z, c))


def to_mirror(value):
    return send(value, lambda x, y, z, c: (x, 3 - y, z, c))


def cost(flops, nbytes):
    return pl.CostEstimate(flops=int(flops) * 64, bytes_accessed=int(nbytes) * 64, transcendentals=0)


def spread(blocks):
    row = lax.broadcasted_iota(jnp.int32, (blocks, blocks * B), 0)
    col = lax.broadcasted_iota(jnp.int32, (blocks, blocks * B), 1)
    return (row == col // B).astype(f32).astype(bf16)


def mask_kernel(blocks, per, mask, w, *rest):
    kept, rows = rest[-2:]
    i = pl.program_id(0)

    @pl.when(i == 0)
    def _():
        rows[...] = jnp.dot(
            mask[...].astype(f32).astype(bf16), spread(blocks), preferred_element_type=f32
        )

    for k in range(per):
        at = slice(k * B, (k + 1) * B)
        kept[at, :] = (w[at, :].astype(f32) * rows[pl.ds(per * i + k, 1), :]).astype(bf16)


def kept_weight(w, mask, *ready):
    rows, cols = w.shape
    steps = 4
    block = pl.BlockSpec((rows // steps, cols), lambda i: (i, 0))
    return pl.pallas_call(
        functools.partial(mask_kernel, cols // B, rows // B // steps),
        grid=(steps,),
        in_specs=[pl.BlockSpec(mask.shape, lambda i: (0, 0)), block]
        + [pl.BlockSpec(memory_space=pl.ANY)] * len(ready),
        out_specs=block,
        out_shape=jax.ShapeDtypeStruct((rows, cols), bf16),
        scratch_shapes=[pltpu.VMEM((rows // B, cols), f32)],
        compiler_params=pltpu.CompilerParams(vmem_limit_bytes=VMEM),
        cost_estimate=cost(0, 18 * MIB),
        name="kept_weight",
    )(mask, w, *ready)


TOKENS_COLUMN = ((0, 0, 64, 0), (1, 0, 64, 64), (2, 0, 64, 128), (3, 0, 32, 192), (4, 0, 32, 224))
TOKENS_SIDE = tuple(
    (3 * s + p, 0, n, 128 * s + dst) for s in range(2) for p, n, dst in ((0, 32, 0), (1, 64, 32), (2, 32, 96))
)
COTANGENTS = (
    (0, 0, 64, 0),
    (1, 32, 64, 64),
    (2, 32, 64, 128),
    (3, 0, 32, 192),
    (4, 0, 32, 224),
    (5, 32, 32, 256),
    (6, 32, 64, 288),
    (7, 0, 32, 352),
    (8, 32, 32, 384),
    (9, 32, 64, 416),
    (10, 0, 32, 480),
)
ANY = pl.BlockSpec(memory_space=pl.ANY)


def collect(table, pieces, rows, sem, out, row, out_sem):
    i = pl.program_id(0)
    keep = pltpu.make_async_copy(rows, out.at[pl.ds(row, rows.shape[0]), :], out_sem)

    @pl.when(i == 0)
    def _():
        moves = [
            pltpu.make_async_copy(pieces[p].at[pl.ds(src, n), :], rows.at[pl.ds(dst, n), :], sem.at[k])
            for k, (p, src, n, dst) in enumerate(table)
        ]
        for move in moves:
            move.start()
        for move in moves:
            move.wait()
        keep.start()

    def finish():
        @pl.when(i == pl.num_programs(0) - 1)
        def _():
            keep.wait()

    return finish


def hidden_kernel(table, n_pieces, half, *refs):
    pieces, uk = refs[:n_pieces], refs[n_pieces]
    pre_out, hid, hid_t, x_out, xs, sem, out_sem = refs[-7:]
    finish = collect(table, pieces, xs, sem, x_out, 256 * half, out_sem)
    pre = jnp.dot(xs[...], uk[...], preferred_element_type=f32)
    pre_out[...] = pre
    h = pre * (0.5 + 0.5 * jnp.tanh(pre * (C + C * 0.044715 * (pre * pre))))
    hid[...] = h.astype(bf16)
    hid_t[...] = h.T.astype(bf16)
    finish()


def hidden_of(half, table, pieces, up_kept, ready, earlier=()):
    n, tile = len(pieces), 512
    across = pl.BlockSpec((256, tile), lambda i: (half, i))
    return pl.pallas_call(
        functools.partial(hidden_kernel, table, n, half),
        grid=(F // tile,),
        in_specs=[ANY] * n
        + [pl.BlockSpec((D, tile), lambda i: (0, i)), ANY]
        + [ANY] * len(earlier),
        out_specs=[across, across, pl.BlockSpec((tile, 256), lambda i: (i, half)), ANY],
        out_shape=[
            jax.ShapeDtypeStruct((512, F), f32),
            jax.ShapeDtypeStruct((512, F), bf16),
            jax.ShapeDtypeStruct((F, 512), bf16),
            jax.ShapeDtypeStruct((512, D), bf16),
        ],
        input_output_aliases={n + 2 + k: k for k in range(len(earlier))},
        scratch_shapes=[
            pltpu.VMEM((256, D), bf16),
            pltpu.SemaphoreType.DMA((len(table),)),
            pltpu.SemaphoreType.DMA,
        ],
        compiler_params=pltpu.CompilerParams(vmem_limit_bytes=VMEM),
        cost_estimate=cost(2 * 256 * D * F, 14 * MIB),
        name="hidden",
    )(*pieces, up_kept, ready, *earlier)


def back_kernel(table, n_pieces, *refs):
    pieces, (dk, pre_ref) = refs[:n_pieces], refs[n_pieces : n_pieces + 2]
    gp, gp_t, d_out, ds, sem, out_sem = refs[-6:]
    finish = collect(table, pieces, ds, sem, d_out, 0, out_sem)
    back = lax.dot_general(ds[...], dk[...], (((1,), (1,)), ((), ())), preferred_element_type=f32)
    pre = pre_ref[...]
    square = pre * pre
    s = 0.5 + 0.5 * jnp.tanh(pre * (C + C * 0.044715 * square))
    g = back * (s + pre * s * (1.0 - s) * (2.0 * C + 6.0 * C * 0.044715 * square))
    gp[...] = g.astype(bf16)
    gp_t[...] = g.T.astype(bf16)
    finish()


def grad_pre_of(pieces, down_kept, pre, ready):
    n, tile = len(pieces), 256
    return pl.pallas_call(
        functools.partial(back_kernel, COTANGENTS, n),
        grid=(F // tile,),
        in_specs=[ANY] * n
        + [
            pl.BlockSpec((tile, D), lambda i: (i, 0)),
            pl.BlockSpec((512, tile), lambda i: (0, i)),
            ANY,
        ],
        out_specs=[
            pl.BlockSpec((512, tile), lambda i: (0, i)),
            pl.BlockSpec((tile, 512), lambda i: (i, 0)),
            ANY,
        ],
        out_shape=[
            jax.ShapeDtypeStruct((512, F), bf16),
            jax.ShapeDtypeStruct((F, 512), bf16),
            jax.ShapeDtypeStruct((512, D), bf16),
        ],
        scratch_shapes=[
            pltpu.VMEM((512, D), bf16),
            pltpu.SemaphoreType.DMA((len(COTANGENTS),)),
            pltpu.SemaphoreType.DMA,
        ],
        compiler_params=pltpu.CompilerParams(vmem_limit_bytes=VMEM),
        cost_estimate=cost(2 * 512 * D * F, 20 * MIB),
        name="grad_pre",
    )(*pieces, down_kept, pre, ready)


def share_kernel(turned, cuts, left, w, _, *outs):
    dims = (((1,), (1 if turned else 0,)), ((), ()))
    total = lax.dot_general(left[...], w[...], dims, preferred_element_type=f32).astype(bf16)
    row = 0
    for out, rows in zip(outs, cuts):
        out[...] = total[row : row + rows, :]
        row += rows


def share(turned, left, block, cuts, w, ready):
    m, tile = sum(cuts), 1024
    return pl.pallas_call(
        functools.partial(share_kernel, turned, cuts),
        grid=(D // tile,),
        in_specs=[
            pl.BlockSpec((m, F), lambda i: (block, 0)),
            pl.BlockSpec((tile, F), lambda i: (i, 0)) if turned else pl.BlockSpec((F, tile), lambda i: (0, i)),
            ANY,
        ],
        out_specs=[pl.BlockSpec((rows, tile), lambda i: (0, i)) for rows in cuts],
        out_shape=[jax.ShapeDtypeStruct((rows, D), bf16) for rows in cuts],
        compiler_params=pltpu.CompilerParams(vmem_limit_bytes=VMEM),
        cost_estimate=cost(2 * m * D * F, 12 * MIB),
        name="share",
    )(left, w, ready)


def row_sums_kernel(plan, n, *refs):
    for out, segments in zip(refs[n + 1 :], plan):
        for k, terms in enumerate(segments):
            total = refs[terms[0]][...].astype(f32)
            for term in terms[1:]:
                total = total + refs[term][...].astype(f32)
            out[32 * k : 32 * (k + 1), :] = total.astype(bf16)


def row_sums(outs, ready):
    arrays, specs, plan = [], [], []
    tile = D // 2
    for segments in outs:
        plan.append([])
        for terms in segments:
            plan[-1].append(range(len(arrays), len(arrays) + len(terms)))
            for array, row in terms:
                arrays.append(array)
                specs.append(pl.BlockSpec((32, tile), lambda i, at=row // 32: (at, i)))
    return pl.pallas_call(
        functools.partial(row_sums_kernel, plan, len(arrays)),
        grid=(D // tile,),
        in_specs=specs + [ANY],
        out_specs=[pl.BlockSpec((32 * len(segments), tile), lambda i: (0, i)) for segments in outs],
        out_shape=[jax.ShapeDtypeStruct((32 * len(segments), D), bf16) for segments in outs],
        compiler_params=pltpu.CompilerParams(vmem_limit_bytes=VMEM),
        cost_estimate=cost(0, 3 * MIB),
        name="row_sums",
    )(*arrays, ready)


def packed_kernel(cuts, added, groups, table, left, right, got, _, *refs):
    outs, (a, b, t, buf, add_buf, a_sem, b_sem, got_sem, out_sem) = refs[: len(cuts)], refs[len(cuts) :]
    first = pltpu.make_async_copy(left, a, a_sem)
    first.start()
    rights = []
    for q in range(8):
        col = pl.multiple_of(groups[q] * 256, 256)
        rights.append(pltpu.make_async_copy(right.at[:, pl.ds(col, 256)], b.at[q], b_sem.at[q]))
        rights[q].start()
    if added:
        more = pltpu.make_async_copy(got, add_buf, got_sem)
        more.start()
    places = [(out, k) for out, n in zip(outs, cuts) for k in range(n)]
    moves = [
        pltpu.make_async_copy(buf.at[q], out.at[k], out_sem.at[q]) for q, (out, k) in enumerate(places)
    ]
    first.wait()
    for q in range(8):
        j = groups[q]
        rights[q].wait()
        base = (q % 2) * 4 * F
        for r in range(0, F, 256):
            acc = jnp.dot(a[r : r + 256, :], b[q], preferred_element_type=f32)
            for ct in range(2):
                part = acc[:, ct * 128 : (ct + 1) * 128]
                row = base + ct * F + r
                t[row : row + 256, :] = part.astype(bf16)
                row += 2 * F
                t[row : row + 256, :] = pltpu.roll(part, 64, 1).astype(bf16)
        for p in range(KEPT // 2):
            ra = pl.multiple_of(base + table[j, 2 * p], B)
            rb = pl.multiple_of(base + table[j, 2 * p + 1], B)
            to = slice(p * B, (p + 1) * B)
            buf[q, to, 0:B] = t[pl.ds(ra, B), 0:B]
            buf[q, to, B : 2 * B] = t[pl.ds(rb, B), B : 2 * B]
        if added:
            if q == 0:
                more.wait()
            buf[q] = (buf[q].astype(f32) + add_buf[q].astype(f32)).astype(bf16)
        moves[q].start()
    for move in moves:
        move.wait()


def packed(groups, table, left, right, ready, cuts=(8,), got=None):
    added = got is not None
    return pl.pallas_call(
        functools.partial(packed_kernel, cuts, added),
        grid_spec=pltpu.PrefetchScalarGridSpec(
            num_scalar_prefetch=2,
            grid=(1,),
            in_specs=[ANY] * 4,
            out_specs=[ANY] * len(cuts),
            scratch_shapes=[
                pltpu.VMEM((F, 512), bf16),
                pltpu.VMEM((8, 512, 256), bf16),
                pltpu.VMEM((8 * F, 128), bf16),
                pltpu.VMEM((8, SLAB, 128), bf16),
                pltpu.VMEM((8, SLAB, 128), bf16),
                pltpu.SemaphoreType.DMA,
                pltpu.SemaphoreType.DMA((8,)),
                pltpu.SemaphoreType.DMA,
                pltpu.SemaphoreType.DMA((8,)),
            ],
        ),
        out_shape=[jax.ShapeDtypeStruct((n, SLAB, 128), bf16) for n in cuts],
        compiler_params=pltpu.CompilerParams(vmem_limit_bytes=VMEM),
        cost_estimate=cost(2 * 512 * F * 2048, 6 * MIB),
        name="packed",
    )(groups, table, left, right, got if added else right, ready)


def expand_kernel(turned, keep, table, w, f, out, s, dense):
    total = w[0].astype(f32) + f[0].astype(f32)
    s[0:SLAB, :] = total
    s[SLAB : 2 * SLAB, :] = pltpu.roll(total, 64, 1)
    target = dense if turned else out
    for r in range(16):
        rows = slice(r * B, (r + 1) * B)
        for c in range(4):
            row = pl.multiple_of(table[r * 4 + c], B)
            half = slice((c % 2) * B, (c % 2 + 1) * B)
            block = s[pl.ds(row, B), half]
            target[rows, c * B : (c + 1) * B] = jnp.where(keep[r * 4 + c] != 0, block, 0.0)
    if turned:
        for r in range(0, F, 128):
            for c in range(0, 256, 128):
                out[c : c + 128, r : r + 128] = dense[r : r + 128, c : c + 128].T


def expand(turned, keep, table, w, f):
    slab = pl.BlockSpec((1, SLAB, 128), lambda i, k, p: (0, 0, 0))
    shape = (256, F) if turned else (F, 256)
    return pl.pallas_call(
        functools.partial(expand_kernel, turned),
        grid_spec=pltpu.PrefetchScalarGridSpec(
            num_scalar_prefetch=2,
            grid=(1,),
            in_specs=[slab, slab],
            out_specs=pl.BlockSpec(shape, lambda i, k, p: (0, 0)),
            scratch_shapes=[pltpu.VMEM((2 * SLAB, 128), f32), pltpu.VMEM((F, 256), f32)],
        ),
        out_shape=jax.ShapeDtypeStruct(shape, f32),
        compiler_params=pltpu.CompilerParams(vmem_limit_bytes=VMEM),
        cost_estimate=cost(0, 2 * MIB),
        name="expand",
    )(keep, table, w, f)


def plan(mask_up, mask_down):
    up = mask_up.reshape(16, 4, 16).transpose(0, 2, 1).reshape(16, 64)
    down = mask_down.reshape(16, 16, 4).transpose(1, 0, 2).reshape(16, 64)
    keep = (jnp.stack([up, down]) != 0).astype(jnp.int32)
    place = jnp.arange(64, dtype=jnp.int32)
    slot = jnp.sum(keep[:, :, None, :] * (place[None, :] < place[:, None]), axis=-1)
    wanted = jnp.arange(KEPT, dtype=jnp.int32)
    hit = (slot[:, :, None, :] == wanted[:, None]) & (keep[:, :, None, :] != 0)
    here = (place // 4) * B + ((place % 4) // 2) * F
    turned = (place % 2) ^ (wanted[:, None] % 2)
    source = jnp.sum(jnp.where(hit, here + turned * (2 * F), 0), axis=-1)
    back = (slot // 2) * B + ((slot % 2) ^ (place % 2)) * SLAB
    return source, jnp.where(keep != 0, back, 0), keep


def add(*terms):
    total = terms[0].astype(f32)
    for term in terms[1:]:
        total = total + term.astype(f32)
    return total.astype(bf16)


def cat(*parts):
    return jnp.concatenate(parts, axis=0)


def stage(*values):
    return lax.optimization_barrier(values)


def local(tokens, w_up, w_down, mask_up, mask_down, cotangent):
    x, d = tokens, cotangent
    dp = lax.axis_index("dp")
    y, xh, c = dp // 4, (dp // 2) % 2, dp % 2

    xm, xp = shift(x, dz=1), shift(x, dz=-1)
    l1, r1 = shift(cat(x[:32], d[:32]), dx=1), shift(cat(x[32:], d[32:]), dx=-1)
    uk = kept_weight(w_up, mask_up)
    table, back, keep = plan(mask_up, mask_down)
    own = [lax.dynamic_index_in_dim(v, dp, 1, keepdims=False) for v in (keep, back)]

    xm, xp, l1, r1, uk, table = stage(xm, xp, l1, r1, uk, table)
    ea, eb = shift(cat(xm[:32], d), dz=1), shift(cat(xp[32:], d), dz=-1)
    l2, r2 = shift(cat(xm[:32], xp[:32]), dx=1), shift(cat(xm[32:], xp[32:]), dx=-1)
    dk = kept_weight(w_down, mask_down, xm)

    ea, eb, l2, r2, dk = stage(ea, eb, l2, r2, dk)
    l3 = shift(cat(ea[:32], ea[32:64], eb[32:64]), dx=1)
    r3 = shift(cat(eb[:32], ea[64:], eb[64:]), dx=-1)
    fa, fb = shift(ea[32:64], dz=1), shift(eb[64:], dz=-1)
    half = hidden_of(0, TOKENS_COLUMN, [x, xm, xp, ea, eb], uk, l2)
    (o_col,) = share(False, half[1], 0, (256,), dk, half[1])

    fa, fb, l3, r3, o_col = stage(fa, fb, l3, r3, o_col)
    l4, r4 = shift(fa, dx=1), shift(fb, dx=-1)
    pre, hid, hid_t, xs = hidden_of(1, TOKENS_SIDE, [l1, l2, l3, r1, r2, r3], uk, o_col, half)
    o_left, o_right = share(False, hid, 1, (128, 128), dk, xs)

    oa, ob = shift(o_left, dx=-1), shift(o_right, dx=1)
    gp, gp_t, ds = grad_pre_of([d, ea, eb, fa, fb, l1, l3, l4, r1, r3, r4], dk, pre, o_left)

    pair, mirror = y ^ 1, 3 - y
    pairs = [(3 - pair, 0), (pair, 0), (mirror ^ 1, 1), (mirror, 1), (mirror, 0), (y, 0), (pair, 1), (y, 1)]
    near = jnp.stack([4 * at + (xh ^ e) * 2 + c for at, e in pairs]).astype(jnp.int32)
    away = near ^ 1
    cuts = (2, 2, 2, 2)

    (up_away,) = packed(away, table[0], gp_t, xs, gp)
    up_got = to_core(up_away)
    t_col, t_left, t_right = share(True, gp, 0, (256, 128, 128), uk, up_away)

    oa, ob, t_col, t_left, t_right = stage(oa, ob, t_col, t_left, t_right)
    ta, tb = shift(t_left, dx=-1), shift(t_right, dx=1)
    (down_away,) = packed(away, table[1], hid_t, ds, t_col)
    down_got = to_core(down_away)
    ua, ub, uc, ud = packed(near, table[0], gp_t, xs, down_away, cuts, up_got)
    u1, u2 = to_pair(ua), to_mirror(ub)
    da, db, dc, dd = packed(near, table[1], hid_t, ds, ud, cuts, down_got)

    ta, tb, dd = stage(ta, tb, dd)
    o, t, a, b, g, h = o_col, t_col, oa, ob, ta, tb
    za, zb = row_sums(
        [
            [[(o, 192), (a, 96)], [(t, 192), (g, 96)]],
            [[(o, 224), (b, 96)], [(t, 224), (h, 96)]],
        ],
        dd,
    )
    da, db, za, zb = stage(da, db, za, zb)
    za, zb = shift(za, dz=1), shift(zb, dz=-1)
    u1, u2, da, db = stage(u1, u2, da, db)
    d1, d2 = to_pair(da), to_mirror(db)

    p, m = row_sums(
        [
            [[(o, 128), (a, 64), (za, 0)], [(o, 160), (b, 64)], [(t, 128), (g, 64), (za, 32)], [(t, 160), (h, 64)]],
            [[(o, 64), (a, 32)], [(o, 96), (b, 32), (zb, 0)], [(t, 64), (g, 32)], [(t, 96), (h, 32), (zb, 32)]],
        ],
        da,
    )
    u1, u2, p, m = stage(u1, u2, p, m)
    p, m = shift(p, dz=1), shift(m, dz=-1)
    u3, u4 = stage(add(uc[0:1], u1[0:1]), add(ud[0:1], u2[0:1]))
    u3, u4 = to_mirror(u3), to_pair(u4)
    d1, d2, dc, _ = stage(d1, d2, dc, u1)
    d3, d4 = to_mirror(add(dc[0:1], d1[0:1])), to_pair(add(dd[0:1], d2[0:1]))

    u3, u4, dc = stage(u3, u4, dc)
    up_far = shift(add(ud[1:2], u2[1:2], u4), dx=2)
    up_near = add(uc[1:2], u1[1:2], u3)
    grad_up = expand(True, own[0][0], own[1][0], up_near, up_far)

    down_far = shift(add(dd[1:2], d2[1:2], d4), dx=2)
    down_near = add(dc[1:2], d1[1:2], d3)
    output, grad_tokens = row_sums(
        [
            [[(o, 0), (a, 0), (p, 0), (m, 0)], [(o, 32), (b, 0), (p, 32), (m, 32)]],
            [[(t, 0), (g, 0), (p, 64), (m, 64)], [(t, 32), (h, 0), (p, 96), (m, 96)]],
        ],
        up_near,
    )
    output, down_near = stage(output, down_near)
    grad_down = expand(False, own[0][1], own[1][1], down_near, down_far)
    return output, grad_tokens, grad_up, grad_down


def solution(mesh):
    placed = (
        P(("dp", "tensor"), None),
        P(None, "tensor"),
        P("tensor", None),
        P(None, "tensor"),
        P("tensor", None),
        P(("dp", "tensor"), None),
    )
    return jax.shard_map(
        local,
        mesh=mesh,
        in_specs=placed,
        out_specs=(
            P(("dp", "tensor"), None),
            P(("dp", "tensor"), None),
            P("dp", "tensor"),
            P("tensor", "dp"),
        ),
        check_vma=False,
    )
```

```python
import functools
import math

import jax
import jax.numpy as jnp
from jax import lax
from jax.experimental import pallas as pl
from jax.experimental.pallas import tpu as pltpu
from jax.sharding import PartitionSpec as P

B = 64
D = 4096
F = 1024
KEPT = 40
SLAB = KEPT // 2 * B
MIB = 1 << 20
VMEM = 60 * MIB
C = math.sqrt(2.0 / math.pi)
f32, bf16 = jnp.float32, jnp.bfloat16
AXES = ("dp", "tensor")


def device_at(x, y, z, c):
    x, y, z = x % 4, y % 4, z % 4
    return ((y * 2 + x // 2) * 2 + c) * 8 + z * 2 + x % 2


def send(value, to):
    pairs = [
        (device_at(x, y, z, c), device_at(*to(x, y, z, c)))
        for x in range(4)
        for y in range(4)
        for z in range(4)
        for c in range(2)
    ]
    return lax.ppermute(value, AXES, pairs)


def shift(value, dx=0, dz=0):
    return send(value, lambda x, y, z, c: (x + dx, y, z + dz, c))


def to_core(value):
    return send(value, lambda x, y, z, c: (x, y, z, 1 - c))


def to_pair(value):
    return send(value, lambda x, y, z, c: (x, y ^ 1, z, c))


def to_mirror(value):
    return send(value, lambda x, y, z, c: (x, 3 - y, z, c))


def cost(flops, nbytes):
    return pl.CostEstimate(flops=int(flops) * 64, bytes_accessed=int(nbytes) * 64, transcendentals=0)


def spread(blocks):
    row = lax.broadcasted_iota(jnp.int32, (blocks, blocks * B), 0)
    col = lax.broadcasted_iota(jnp.int32, (blocks, blocks * B), 1)
    return (row == col // B).astype(f32).astype(bf16)


def mask_kernel(blocks, per, mask, w, *rest):
    kept, rows = rest[-2:]
    i = pl.program_id(0)

    @pl.when(i == 0)
    def _():
        rows[...] = jnp.dot(
            mask[...].astype(f32).astype(bf16), spread(blocks), preferred_element_type=f32
        )

    for k in range(per):
        at = slice(k * B, (k + 1) * B)
        kept[at, :] = (w[at, :].astype(f32) * rows[pl.ds(per * i + k, 1), :]).astype(bf16)


def kept_weight(w, mask, *ready):
    rows, cols = w.shape
    steps = 4
    block = pl.BlockSpec((rows // steps, cols), lambda i: (i, 0))
    return pl.pallas_call(
        functools.partial(mask_kernel, cols // B, rows // B // steps),
        grid=(steps,),
        in_specs=[pl.BlockSpec(mask.shape, lambda i: (0, 0)), block]
        + [pl.BlockSpec(memory_space=pl.ANY)] * len(ready),
        out_specs=block,
        out_shape=jax.ShapeDtypeStruct((rows, cols), bf16),
        scratch_shapes=[pltpu.VMEM((rows // B, cols), f32)],
        compiler_params=pltpu.CompilerParams(vmem_limit_bytes=VMEM),
        cost_estimate=cost(0, 18 * MIB),
        name="kept_weight",
    )(mask, w, *ready)


TOKENS_COLUMN = ((0, 0, 64, 0), (1, 0, 64, 64), (2, 0, 64, 128), (3, 0, 32, 192), (4, 0, 32, 224))
TOKENS_SIDE = tuple(
    (3 * s + p, 0, n, 128 * s + dst) for s in range(2) for p, n, dst in ((0, 32, 0), (1, 64, 32), (2, 32, 96))
)
COTANGENTS = (
    (0, 0, 64, 0),
    (1, 32, 64, 64),
    (2, 32, 64, 128),
    (3, 0, 32, 192),
    (4, 0, 32, 224),
    (5, 32, 32, 256),
    (6, 32, 64, 288),
    (7, 0, 32, 352),
    (8, 32, 32, 384),
    (9, 32, 64, 416),
    (10, 0, 32, 480),
)
ANY = pl.BlockSpec(memory_space=pl.ANY)


def collect(table, pieces, rows, sem, out, row, out_sem):
    i = pl.program_id(0)
    keep = pltpu.make_async_copy(rows, out.at[pl.ds(row, rows.shape[0]), :], out_sem)

    @pl.when(i == 0)
    def _():
        moves = [
            pltpu.make_async_copy(pieces[p].at[pl.ds(src, n), :], rows.at[pl.ds(dst, n), :], sem.at[k])
            for k, (p, src, n, dst) in enumerate(table)
        ]
        for move in moves:
            move.start()
        for move in moves:
            move.wait()
        keep.start()

    def finish():
        @pl.when(i == pl.num_programs(0) - 1)
        def _():
            keep.wait()

    return finish


def hidden_kernel(table, n_pieces, half, *refs):
    pieces, uk = refs[:n_pieces], refs[n_pieces]
    pre_out, hid, hid_t, x_out, xs, sem, out_sem = refs[-7:]
    finish = collect(table, pieces, xs, sem, x_out, 256 * half, out_sem)
    pre = jnp.dot(xs[...], uk[...], preferred_element_type=f32)
    pre_out[...] = pre
    h = pre * (0.5 + 0.5 * jnp.tanh(pre * (C + C * 0.044715 * (pre * pre))))
    hid[...] = h.astype(bf16)
    hid_t[...] = h.T.astype(bf16)
    finish()


def hidden_of(half, table, pieces, up_kept, ready, earlier=()):
    n, tile = len(pieces), 512
    across = pl.BlockSpec((256, tile), lambda i: (half, i))
    return pl.pallas_call(
        functools.partial(hidden_kernel, table, n, half),
        grid=(F // tile,),
        in_specs=[ANY] * n
        + [pl.BlockSpec((D, tile), lambda i: (0, i)), ANY]
        + [ANY] * len(earlier),
        out_specs=[across, across, pl.BlockSpec((tile, 256), lambda i: (i, half)), ANY],
        out_shape=[
            jax.ShapeDtypeStruct((512, F), f32),
            jax.ShapeDtypeStruct((512, F), bf16),
            jax.ShapeDtypeStruct((F, 512), bf16),
            jax.ShapeDtypeStruct((512, D), bf16),
        ],
        input_output_aliases={n + 2 + k: k for k in range(len(earlier))},
        scratch_shapes=[
            pltpu.VMEM((256, D), bf16),
            pltpu.SemaphoreType.DMA((len(table),)),
            pltpu.SemaphoreType.DMA,
        ],
        compiler_params=pltpu.CompilerParams(vmem_limit_bytes=VMEM),
        cost_estimate=cost(2 * 256 * D * F, 14 * MIB),
        name="hidden",
    )(*pieces, up_kept, ready, *earlier)


def back_kernel(table, n_pieces, *refs):
    pieces, (dk, pre_ref) = refs[:n_pieces], refs[n_pieces : n_pieces + 2]
    gp, gp_t, d_out, ds, sem, out_sem = refs[-6:]
    finish = collect(table, pieces, ds, sem, d_out, 0, out_sem)
    back = lax.dot_general(ds[...], dk[...], (((1,), (1,)), ((), ())), preferred_element_type=f32)
    pre = pre_ref[...]
    square = pre * pre
    s = 0.5 + 0.5 * jnp.tanh(pre * (C + C * 0.044715 * square))
    g = back * (s + pre * s * (1.0 - s) * (2.0 * C + 6.0 * C * 0.044715 * square))
    gp[...] = g.astype(bf16)
    gp_t[...] = g.T.astype(bf16)
    finish()


def grad_pre_of(pieces, down_kept, pre, ready):
    n, tile = len(pieces), 256
    return pl.pallas_call(
        functools.partial(back_kernel, COTANGENTS, n),
        grid=(F // tile,),
        in_specs=[ANY] * n
        + [
            pl.BlockSpec((tile, D), lambda i: (i, 0)),
            pl.BlockSpec((512, tile), lambda i: (0, i)),
            ANY,
        ],
        out_specs=[
            pl.BlockSpec((512, tile), lambda i: (0, i)),
            pl.BlockSpec((tile, 512), lambda i: (i, 0)),
            ANY,
        ],
        out_shape=[
            jax.ShapeDtypeStruct((512, F), bf16),
            jax.ShapeDtypeStruct((F, 512), bf16),
            jax.ShapeDtypeStruct((512, D), bf16),
        ],
        scratch_shapes=[
            pltpu.VMEM((512, D), bf16),
            pltpu.SemaphoreType.DMA((len(COTANGENTS),)),
            pltpu.SemaphoreType.DMA,
        ],
        compiler_params=pltpu.CompilerParams(vmem_limit_bytes=VMEM),
        cost_estimate=cost(2 * 512 * D * F, 20 * MIB),
        name="grad_pre",
    )(*pieces, down_kept, pre, ready)


def share_kernel(turned, cuts, left, w, _, *outs):
    dims = (((1,), (1 if turned else 0,)), ((), ()))
    total = lax.dot_general(left[...], w[...], dims, preferred_element_type=f32).astype(bf16)
    row = 0
    for out, rows in zip(outs, cuts):
        out[...] = total[row : row + rows, :]
        row += rows


def share(turned, left, block, cuts, w, ready):
    m, tile = sum(cuts), 1024
    return pl.pallas_call(
        functools.partial(share_kernel, turned, cuts),
        grid=(D // tile,),
        in_specs=[
            pl.BlockSpec((m, F), lambda i: (block, 0)),
            pl.BlockSpec((tile, F), lambda i: (i, 0)) if turned else pl.BlockSpec((F, tile), lambda i: (0, i)),
            ANY,
        ],
        out_specs=[pl.BlockSpec((rows, tile), lambda i: (0, i)) for rows in cuts],
        out_shape=[jax.ShapeDtypeStruct((rows, D), bf16) for rows in cuts],
        compiler_params=pltpu.CompilerParams(vmem_limit_bytes=VMEM),
        cost_estimate=cost(2 * m * D * F, 12 * MIB),
        name="share",
    )(left, w, ready)


def row_sums_kernel(plan, n, *refs):
    for out, segments in zip(refs[n + 1 :], plan):
        for k, terms in enumerate(segments):
            total = refs[terms[0]][...].astype(f32)
            for term in terms[1:]:
                total = total + refs[term][...].astype(f32)
            out[32 * k : 32 * (k + 1), :] = total.astype(bf16)


def row_sums(outs, ready):
    arrays, specs, plan = [], [], []
    tile = D // 2
    for segments in outs:
        plan.append([])
        for terms in segments:
            plan[-1].append(range(len(arrays), len(arrays) + len(terms)))
            for array, row in terms:
                arrays.append(array)
                specs.append(pl.BlockSpec((32, tile), lambda i, at=row // 32: (at, i)))
    return pl.pallas_call(
        functools.partial(row_sums_kernel, plan, len(arrays)),
        grid=(D // tile,),
        in_specs=specs + [ANY],
        out_specs=[pl.BlockSpec((32 * len(segments), tile), lambda i: (0, i)) for segments in outs],
        out_shape=[jax.ShapeDtypeStruct((32 * len(segments), D), bf16) for segments in outs],
        compiler_params=pltpu.CompilerParams(vmem_limit_bytes=VMEM),
        cost_estimate=cost(0, 3 * MIB),
        name="row_sums",
    )(*arrays, ready)


def packed_kernel(cuts, added, groups, table, left, right, got, _, *refs):
    outs, (a, b, t, buf, add_buf, a_sem, b_sem, got_sem, out_sem) = refs[: len(cuts)], refs[len(cuts) :]
    first = pltpu.make_async_copy(left, a, a_sem)
    first.start()
    rights = []
    for q in range(8):
        col = pl.multiple_of(groups[q] * 256, 256)
        rights.append(pltpu.make_async_copy(right.at[:, pl.ds(col, 256)], b.at[q], b_sem.at[q]))
        rights[q].start()
    if added:
        more = pltpu.make_async_copy(got, add_buf, got_sem)
        more.start()
    places = [(out, k) for out, n in zip(outs, cuts) for k in range(n)]
    moves = [
        pltpu.make_async_copy(buf.at[q], out.at[k], out_sem.at[q]) for q, (out, k) in enumerate(places)
    ]
    first.wait()
    for q in range(8):
        j = groups[q]
        rights[q].wait()
        base = (q % 2) * 4 * F
        for r in range(0, F, 256):
            acc = jnp.dot(a[r : r + 256, :], b[q], preferred_element_type=f32)
            for ct in range(2):
                part = acc[:, ct * 128 : (ct + 1) * 128]
                row = base + ct * F + r
                t[row : row + 256, :] = part.astype(bf16)
                row += 2 * F
                t[row : row + 256, :] = pltpu.roll(part, 64, 1).astype(bf16)
        for p in range(KEPT // 2):
            ra = pl.multiple_of(base + table[j, 2 * p], B)
            rb = pl.multiple_of(base + table[j, 2 * p + 1], B)
            to = slice(p * B, (p + 1) * B)
            buf[q, to, 0:B] = t[pl.ds(ra, B), 0:B]
            buf[q, to, B : 2 * B] = t[pl.ds(rb, B), B : 2 * B]
        if added:
            if q == 0:
                more.wait()
            buf[q] = (buf[q].astype(f32) + add_buf[q].astype(f32)).astype(bf16)
        moves[q].start()
    for move in moves:
        move.wait()


def packed(groups, table, left, right, ready, cuts=(8,), got=None):
    added = got is not None
    return pl.pallas_call(
        functools.partial(packed_kernel, cuts, added),
        grid_spec=pltpu.PrefetchScalarGridSpec(
            num_scalar_prefetch=2,
            grid=(1,),
            in_specs=[ANY] * 4,
            out_specs=[ANY] * len(cuts),
            scratch_shapes=[
                pltpu.VMEM((F, 512), bf16),
                pltpu.VMEM((8, 512, 256), bf16),
                pltpu.VMEM((8 * F, 128), bf16),
                pltpu.VMEM((8, SLAB, 128), bf16),
                pltpu.VMEM((8, SLAB, 128), bf16),
                pltpu.SemaphoreType.DMA,
                pltpu.SemaphoreType.DMA((8,)),
                pltpu.SemaphoreType.DMA,
                pltpu.SemaphoreType.DMA((8,)),
            ],
        ),
        out_shape=[jax.ShapeDtypeStruct((n, SLAB, 128), bf16) for n in cuts],
        compiler_params=pltpu.CompilerParams(vmem_limit_bytes=VMEM),
        cost_estimate=cost(2 * 512 * F * 2048, 6 * MIB),
        name="packed",
    )(groups, table, left, right, got if added else right, ready)


def expand_kernel(turned, keep, table, w, f, out, s, dense):
    total = w[0].astype(f32) + f[0].astype(f32)
    s[0:SLAB, :] = total
    s[SLAB : 2 * SLAB, :] = pltpu.roll(total, 64, 1)
    target = dense if turned else out
    for r in range(16):
        rows = slice(r * B, (r + 1) * B)
        for c in range(4):
            row = pl.multiple_of(table[r * 4 + c], B)
            half = slice((c % 2) * B, (c % 2 + 1) * B)
            block = s[pl.ds(row, B), half]
            target[rows, c * B : (c + 1) * B] = jnp.where(keep[r * 4 + c] != 0, block, 0.0)
    if turned:
        for r in range(0, F, 128):
            for c in range(0, 256, 128):
                out[c : c + 128, r : r + 128] = dense[r : r + 128, c : c + 128].T


def expand(turned, keep, table, w, f):
    slab = pl.BlockSpec((1, SLAB, 128), lambda i, k, p: (0, 0, 0))
    shape = (256, F) if turned else (F, 256)
    return pl.pallas_call(
        functools.partial(expand_kernel, turned),
        grid_spec=pltpu.PrefetchScalarGridSpec(
            num_scalar_prefetch=2,
            grid=(1,),
            in_specs=[slab, slab],
            out_specs=pl.BlockSpec(shape, lambda i, k, p: (0, 0)),
            scratch_shapes=[pltpu.VMEM((2 * SLAB, 128), f32), pltpu.VMEM((F, 256), f32)],
        ),
        out_shape=jax.ShapeDtypeStruct(shape, f32),
        compiler_params=pltpu.CompilerParams(vmem_limit_bytes=VMEM),
        cost_estimate=cost(0, 2 * MIB),
        name="expand",
    )(keep, table, w, f)


def plan(mask_up, mask_down):
    up = mask_up.reshape(16, 4, 16).transpose(0, 2, 1).reshape(16, 64)
    down = mask_down.reshape(16, 16, 4).transpose(1, 0, 2).reshape(16, 64)
    keep = (jnp.stack([up, down]) != 0).astype(jnp.int32)
    place = jnp.arange(64, dtype=jnp.int32)
    slot = jnp.sum(keep[:, :, None, :] * (place[None, :] < place[:, None]), axis=-1)
    wanted = jnp.arange(KEPT, dtype=jnp.int32)
    hit = (slot[:, :, None, :] == wanted[:, None]) & (keep[:, :, None, :] != 0)
    here = (place // 4) * B + ((place % 4) // 2) * F
    turned = (place % 2) ^ (wanted[:, None] % 2)
    source = jnp.sum(jnp.where(hit, here + turned * (2 * F), 0), axis=-1)
    back = (slot // 2) * B + ((slot % 2) ^ (place % 2)) * SLAB
    return source, jnp.where(keep != 0, back, 0), keep


def add(*terms):
    total = terms[0].astype(f32)
    for term in terms[1:]:
        total = total + term.astype(f32)
    return total.astype(bf16)


def cat(*parts):
    return jnp.concatenate(parts, axis=0)


def stage(*values):
    return lax.optimization_barrier(values)


def local(tokens, w_up, w_down, mask_up, mask_down, cotangent):
    x, d = tokens, cotangent
    dp = lax.axis_index("dp")
    y, xh, c = dp // 4, (dp // 2) % 2, dp % 2

    xm, xp = shift(x, dz=1), shift(x, dz=-1)
    l1, r1 = shift(cat(x[:32], d[:32]), dx=1), shift(cat(x[32:], d[32:]), dx=-1)
    uk = kept_weight(w_up, mask_up)
    table, back, keep = plan(mask_up, mask_down)
    own = [lax.dynamic_index_in_dim(v, dp, 1, keepdims=False) for v in (keep, back)]

    xm, xp, l1, r1, uk, table = stage(xm, xp, l1, r1, uk, table)
    ea, eb = shift(cat(xm[:32], d), dz=1), shift(cat(xp[32:], d), dz=-1)
    l2, r2 = shift(cat(xm[:32], xp[:32]), dx=1), shift(cat(xm[32:], xp[32:]), dx=-1)
    dk = kept_weight(w_down, mask_down, xm)

    ea, eb, l2, r2, dk = stage(ea, eb, l2, r2, dk)
    l3 = shift(cat(ea[:32], ea[32:64], eb[32:64]), dx=1)
    r3 = shift(cat(eb[:32], ea[64:], eb[64:]), dx=-1)
    fa, fb = shift(ea[32:64], dz=1), shift(eb[64:], dz=-1)
    half = hidden_of(0, TOKENS_COLUMN, [x, xm, xp, ea, eb], uk, l2)
    (o_col,) = share(False, half[1], 0, (256,), dk, half[1])

    fa, fb, l3, r3, o_col = stage(fa, fb, l3, r3, o_col)
    l4, r4 = shift(fa, dx=1), shift(fb, dx=-1)
    pre, hid, hid_t, xs = hidden_of(1, TOKENS_SIDE, [l1, l2, l3, r1, r2, r3], uk, o_col, half)
    o_left, o_right = share(False, hid, 1, (128, 128), dk, xs)

    oa, ob = shift(o_left, dx=-1), shift(o_right, dx=1)
    gp, gp_t, ds = grad_pre_of([d, ea, eb, fa, fb, l1, l3, l4, r1, r3, r4], dk, pre, o_left)

    pair, mirror = y ^ 1, 3 - y
    pairs = [(3 - pair, 0), (pair, 0), (mirror ^ 1, 1), (mirror, 1), (mirror, 0), (y, 0), (pair, 1), (y, 1)]
    near = jnp.stack([4 * at + (xh ^ e) * 2 + c for at, e in pairs]).astype(jnp.int32)
    away = near ^ 1
    cuts = (2, 2, 2, 2)

    (up_away,) = packed(away, table[0], gp_t, xs, gp)
    up_got = to_core(up_away)
    t_col, t_left, t_right = share(True, gp, 0, (256, 128, 128), uk, up_away)

    oa, ob, t_col, t_left, t_right = stage(oa, ob, t_col, t_left, t_right)
    ta, tb = shift(t_left, dx=-1), shift(t_right, dx=1)
    (down_away,) = packed(away, table[1], hid_t, ds, t_col)
    down_got = to_core(down_away)
    ua, ub, uc, ud = packed(near, table[0], gp_t, xs, down_away, cuts, up_got)
    u1, u2 = to_pair(ua), to_mirror(ub)
    da, db, dc, dd = packed(near, table[1], hid_t, ds, ud, cuts, down_got)

    ta, tb, dd = stage(ta, tb, dd)
    o, t, a, b, g, h = o_col, t_col, oa, ob, ta, tb
    za, zb = row_sums(
        [
            [[(o, 192), (a, 96)], [(t, 192), (g, 96)]],
            [[(o, 224), (b, 96)], [(t, 224), (h, 96)]],
        ],
        dd,
    )
    da, db, za, zb = stage(da, db, za, zb)
    za, zb = shift(za, dz=1), shift(zb, dz=-1)
    u1, u2, da, db = stage(u1, u2, da, db)
    d1, d2 = to_pair(da), to_mirror(db)

    p, m = row_sums(
        [
            [[(o, 128), (a, 64), (za, 0)], [(o, 160), (b, 64)], [(t, 128), (g, 64), (za, 32)], [(t, 160), (h, 64)]],
            [[(o, 64), (a, 32)], [(o, 96), (b, 32), (zb, 0)], [(t, 64), (g, 32)], [(t, 96), (h, 32), (zb, 32)]],
        ],
        da,
    )
    u1, u2, p, m = stage(u1, u2, p, m)
    p, m = shift(p, dz=1), shift(m, dz=-1)
    u3, u4 = stage(add(uc[0:1], u1[0:1]), add(ud[0:1], u2[0:1]))
    u3, u4 = to_mirror(u3), to_pair(u4)
    d1, d2, dc, _ = stage(d1, d2, dc, u1)
    d3, d4 = to_mirror(add(dc[0:1], d1[0:1])), to_pair(add(dd[0:1], d2[0:1]))

    u3, u4, dc = stage(u3, u4, dc)
    up_far = shift(add(ud[1:2], u2[1:2], u4), dx=2)
    up_near = add(uc[1:2], u1[1:2], u3)
    grad_up = expand(True, own[0][0], own[1][0], up_near, up_far)

    down_far = shift(add(dd[1:2], d2[1:2], d4), dx=2)
    down_near = add(dc[1:2], d1[1:2], d3)
    output, grad_tokens = row_sums(
        [
            [[(o, 0), (a, 0), (p, 0), (m, 0)], [(o, 32), (b, 0), (p, 32), (m, 32)]],
            [[(t, 0), (g, 0), (p, 64), (m, 64)], [(t, 32), (h, 0), (p, 96), (m, 96)]],
        ],
        up_near,
    )
    output, down_near = stage(output, down_near)
    grad_down = expand(False, own[0][1], own[1][1], down_near, down_far)
    return output, grad_tokens, grad_up, grad_down


def solution(mesh):
    placed = (
        P(("dp", "tensor"), None),
        P(None, "tensor"),
        P("tensor", None),
        P(None, "tensor"),
        P("tensor", None),
        P(("dp", "tensor"), None),
    )
    return jax.shard_map(
        local,
        mesh=mesh,
        in_specs=placed,
        out_specs=(
            P(("dp", "tensor"), None),
            P(("dp", "tensor"), None),
            P("dp", "tensor"),
            P("tensor", "dp"),
        ),
        check_vma=False,
    )
```

```python
import functools
import math

import jax
import jax.numpy as jnp
from jax import lax
from jax.experimental import pallas as pl
from jax.experimental.pallas import tpu as pltpu
from jax.sharding import PartitionSpec as P

B = 64
D = 4096
F = 1024
KEPT = 40
SLAB = KEPT // 2 * B
MIB = 1 << 20
VMEM = 60 * MIB
C = math.sqrt(2.0 / math.pi)
f32, bf16 = jnp.float32, jnp.bfloat16
AXES = ("dp", "tensor")


def device_at(x, y, z, c):
    x, y, z = x % 4, y % 4, z % 4
    return ((y * 2 + x // 2) * 2 + c) * 8 + z * 2 + x % 2


def send(value, to):
    pairs = [
        (device_at(x, y, z, c), device_at(*to(x, y, z, c)))
        for x in range(4)
        for y in range(4)
        for z in range(4)
        for c in range(2)
    ]
    return lax.ppermute(value, AXES, pairs)


def shift(value, dx=0, dz=0):
    return send(value, lambda x, y, z, c: (x + dx, y, z + dz, c))


def to_core(value):
    return send(value, lambda x, y, z, c: (x, y, z, 1 - c))


def to_pair(value):
    return send(value, lambda x, y, z, c: (x, y ^ 1, z, c))


def to_mirror(value):
    return send(value, lambda x, y, z, c: (x, 3 - y, z, c))


def cost(flops, nbytes):
    return pl.CostEstimate(flops=int(flops) * 64, bytes_accessed=int(nbytes) * 64, transcendentals=0)


def spread(blocks):
    row = lax.broadcasted_iota(jnp.int32, (blocks, blocks * B), 0)
    col = lax.broadcasted_iota(jnp.int32, (blocks, blocks * B), 1)
    return (row == col // B).astype(f32).astype(bf16)


def mask_kernel(blocks, per, mask, w, *rest):
    kept, rows = rest[-2:]
    i = pl.program_id(0)

    @pl.when(i == 0)
    def _():
        rows[...] = jnp.dot(
            mask[...].astype(f32).astype(bf16), spread(blocks), preferred_element_type=f32
        )

    for k in range(per):
        at = slice(k * B, (k + 1) * B)
        kept[at, :] = (w[at, :].astype(f32) * rows[pl.ds(per * i + k, 1), :]).astype(bf16)


def kept_weight(w, mask, *ready):
    rows, cols = w.shape
    steps = 4
    block = pl.BlockSpec((rows // steps, cols), lambda i: (i, 0))
    return pl.pallas_call(
        functools.partial(mask_kernel, cols // B, rows // B // steps),
        grid=(steps,),
        in_specs=[pl.BlockSpec(mask.shape, lambda i: (0, 0)), block]
        + [pl.BlockSpec(memory_space=pl.ANY)] * len(ready),
        out_specs=block,
        out_shape=jax.ShapeDtypeStruct((rows, cols), bf16),
        scratch_shapes=[pltpu.VMEM((rows // B, cols), f32)],
        compiler_params=pltpu.CompilerParams(vmem_limit_bytes=VMEM),
        cost_estimate=cost(0, 18 * MIB),
        name="kept_weight",
    )(mask, w, *ready)


TOKENS_COLUMN = ((0, 0, 64, 0), (1, 0, 64, 64), (2, 0, 64, 128), (3, 0, 32, 192), (4, 0, 32, 224))
TOKENS_SIDE = tuple(
    (3 * s + p, 0, n, 128 * s + dst) for s in range(2) for p, n, dst in ((0, 32, 0), (1, 64, 32), (2, 32, 96))
)
COTANGENTS = (
    (0, 0, 64, 0),
    (1, 32, 64, 64),
    (2, 32, 64, 128),
    (3, 0, 32, 192),
    (4, 0, 32, 224),
    (5, 32, 32, 256),
    (6, 32, 64, 288),
    (7, 0, 32, 352),
    (8, 32, 32, 384),
    (9, 32, 64, 416),
    (10, 0, 32, 480),
)
ANY = pl.BlockSpec(memory_space=pl.ANY)


def collect(table, pieces, rows, sem, out, row, out_sem):
    i = pl.program_id(0)
    keep = pltpu.make_async_copy(rows, out.at[pl.ds(row, rows.shape[0]), :], out_sem)

    @pl.when(i == 0)
    def _():
        moves = [
            pltpu.make_async_copy(pieces[p].at[pl.ds(src, n), :], rows.at[pl.ds(dst, n), :], sem.at[k])
            for k, (p, src, n, dst) in enumerate(table)
        ]
        for move in moves:
            move.start()
        for move in moves:
            move.wait()
        keep.start()

    def finish():
        @pl.when(i == pl.num_programs(0) - 1)
        def _():
            keep.wait()

    return finish


def hidden_kernel(table, n_pieces, half, *refs):
    pieces, uk = refs[:n_pieces], refs[n_pieces]
    pre_out, hid, hid_t, x_out, xs, sem, out_sem = refs[-7:]
    finish = collect(table, pieces, xs, sem, x_out, 256 * half, out_sem)
    pre = jnp.dot(xs[...], uk[...], preferred_element_type=f32)
    pre_out[...] = pre
    h = pre * (0.5 + 0.5 * jnp.tanh(pre * (C + C * 0.044715 * (pre * pre))))
    hid[...] = h.astype(bf16)
    hid_t[...] = h.T.astype(bf16)
    finish()


def hidden_of(half, table, pieces, up_kept, ready, earlier=()):
    n, tile = len(pieces), 512
    across = pl.BlockSpec((256, tile), lambda i: (half, i))
    return pl.pallas_call(
        functools.partial(hidden_kernel, table, n, half),
        grid=(F // tile,),
        in_specs=[ANY] * n
        + [pl.BlockSpec((D, tile), lambda i: (0, i)), ANY]
        + [ANY] * len(earlier),
        out_specs=[across, across, pl.BlockSpec((tile, 256), lambda i: (i, half)), ANY],
        out_shape=[
            jax.ShapeDtypeStruct((512, F), f32),
            jax.ShapeDtypeStruct((512, F), bf16),
            jax.ShapeDtypeStruct((F, 512), bf16),
            jax.ShapeDtypeStruct((512, D), bf16),
        ],
        input_output_aliases={n + 2 + k: k for k in range(len(earlier))},
        scratch_shapes=[
            pltpu.VMEM((256, D), bf16),
            pltpu.SemaphoreType.DMA((len(table),)),
            pltpu.SemaphoreType.DMA,
        ],
        compiler_params=pltpu.CompilerParams(vmem_limit_bytes=VMEM),
        cost_estimate=cost(2 * 256 * D * F, 14 * MIB),
        name="hidden",
    )(*pieces, up_kept, ready, *earlier)


def back_kernel(table, n_pieces, *refs):
    pieces, (dk, pre_ref) = refs[:n_pieces], refs[n_pieces : n_pieces + 2]
    gp, gp_t, d_out, ds, sem, out_sem = refs[-6:]
    finish = collect(table, pieces, ds, sem, d_out, 0, out_sem)
    back = lax.dot_general(ds[...], dk[...], (((1,), (1,)), ((), ())), preferred_element_type=f32)
    pre = pre_ref[...]
    square = pre * pre
    s = 0.5 + 0.5 * jnp.tanh(pre * (C + C * 0.044715 * square))
    g = back * (s + pre * s * (1.0 - s) * (2.0 * C + 6.0 * C * 0.044715 * square))
    gp[...] = g.astype(bf16)
    gp_t[...] = g.T.astype(bf16)
    finish()


def grad_pre_of(pieces, down_kept, pre, ready):
    n, tile = len(pieces), 256
    return pl.pallas_call(
        functools.partial(back_kernel, COTANGENTS, n),
        grid=(F // tile,),
        in_specs=[ANY] * n
        + [
            pl.BlockSpec((tile, D), lambda i: (i, 0)),
            pl.BlockSpec((512, tile), lambda i: (0, i)),
            ANY,
        ],
        out_specs=[
            pl.BlockSpec((512, tile), lambda i: (0, i)),
            pl.BlockSpec((tile, 512), lambda i: (i, 0)),
            ANY,
        ],
        out_shape=[
            jax.ShapeDtypeStruct((512, F), bf16),
            jax.ShapeDtypeStruct((F, 512), bf16),
            jax.ShapeDtypeStruct((512, D), bf16),
        ],
        scratch_shapes=[
            pltpu.VMEM((512, D), bf16),
            pltpu.SemaphoreType.DMA((len(COTANGENTS),)),
            pltpu.SemaphoreType.DMA,
        ],
        compiler_params=pltpu.CompilerParams(vmem_limit_bytes=VMEM),
        cost_estimate=cost(2 * 512 * D * F, 20 * MIB),
        name="grad_pre",
    )(*pieces, down_kept, pre, ready)


def share_kernel(turned, cuts, left, w, _, *outs):
    dims = (((1,), (1 if turned else 0,)), ((), ()))
    total = lax.dot_general(left[...], w[...], dims, preferred_element_type=f32).astype(bf16)
    row = 0
    for out, rows in zip(outs, cuts):
        out[...] = total[row : row + rows, :]
        row += rows


def share(turned, left, block, cuts, w, ready):
    m, tile = sum(cuts), 1024
    return pl.pallas_call(
        functools.partial(share_kernel, turned, cuts),
        grid=(D // tile,),
        in_specs=[
            pl.BlockSpec((m, F), lambda i: (block, 0)),
            pl.BlockSpec((tile, F), lambda i: (i, 0)) if turned else pl.BlockSpec((F, tile), lambda i: (0, i)),
            ANY,
        ],
        out_specs=[pl.BlockSpec((rows, tile), lambda i: (0, i)) for rows in cuts],
        out_shape=[jax.ShapeDtypeStruct((rows, D), bf16) for rows in cuts],
        compiler_params=pltpu.CompilerParams(vmem_limit_bytes=VMEM),
        cost_estimate=cost(2 * m * D * F, 12 * MIB),
        name="share",
    )(left, w, ready)


def row_sums_kernel(plan, n, *refs):
    for out, segments in zip(refs[n + 1 :], plan):
        for k, terms in enumerate(segments):
            total = refs[terms[0]][...].astype(f32)
            for term in terms[1:]:
                total = total + refs[term][...].astype(f32)
            out[32 * k : 32 * (k + 1), :] = total.astype(bf16)


def row_sums(outs, ready):
    arrays, specs, plan = [], [], []
    tile = D // 2
    for segments in outs:
        plan.append([])
        for terms in segments:
            plan[-1].append(range(len(arrays), len(arrays) + len(terms)))
            for array, row in terms:
                arrays.append(array)
                specs.append(pl.BlockSpec((32, tile), lambda i, at=row // 32: (at, i)))
    return pl.pallas_call(
        functools.partial(row_sums_kernel, plan, len(arrays)),
        grid=(D // tile,),
        in_specs=specs + [ANY],
        out_specs=[pl.BlockSpec((32 * len(segments), tile), lambda i: (0, i)) for segments in outs],
        out_shape=[jax.ShapeDtypeStruct((32 * len(segments), D), bf16) for segments in outs],
        compiler_params=pltpu.CompilerParams(vmem_limit_bytes=VMEM),
        cost_estimate=cost(0, 3 * MIB),
        name="row_sums",
    )(*arrays, ready)


def packed_kernel(cuts, added, groups, table, left, right, got, _, *refs):
    outs, (a, b, t, buf, add_buf, a_sem, b_sem, got_sem, out_sem) = refs[: len(cuts)], refs[len(cuts) :]
    first = pltpu.make_async_copy(left, a, a_sem)
    first.start()
    rights = []
    for q in range(8):
        col = pl.multiple_of(groups[q] * 256, 256)
        rights.append(pltpu.make_async_copy(right.at[:, pl.ds(col, 256)], b.at[q], b_sem.at[q]))
        rights[q].start()
    if added:
        more = pltpu.make_async_copy(got, add_buf, got_sem)
        more.start()
    places = [(out, k) for out, n in zip(outs, cuts) for k in range(n)]
    moves = [
        pltpu.make_async_copy(buf.at[q], out.at[k], out_sem.at[q]) for q, (out, k) in enumerate(places)
    ]
    first.wait()
    for q in range(8):
        j = groups[q]
        rights[q].wait()
        base = (q % 2) * 4 * F
        for r in range(0, F, 256):
            acc = jnp.dot(a[r : r + 256, :], b[q], preferred_element_type=f32)
            for ct in range(2):
                part = acc[:, ct * 128 : (ct + 1) * 128]
                row = base + ct * F + r
                t[row : row + 256, :] = part.astype(bf16)
                row += 2 * F
                t[row : row + 256, :] = pltpu.roll(part, 64, 1).astype(bf16)
        for p in range(KEPT // 2):
            ra = pl.multiple_of(base + table[j, 2 * p], B)
            rb = pl.multiple_of(base + table[j, 2 * p + 1], B)
            to = slice(p * B, (p + 1) * B)
            buf[q, to, 0:B] = t[pl.ds(ra, B), 0:B]
            buf[q, to, B : 2 * B] = t[pl.ds(rb, B), B : 2 * B]
        if added:
            if q == 0:
                more.wait()
            buf[q] = (buf[q].astype(f32) + add_buf[q].astype(f32)).astype(bf16)
        moves[q].start()
    for move in moves:
        move.wait()


def packed(groups, table, left, right, ready, cuts=(8,), got=None):
    added = got is not None
    return pl.pallas_call(
        functools.partial(packed_kernel, cuts, added),
        grid_spec=pltpu.PrefetchScalarGridSpec(
            num_scalar_prefetch=2,
            grid=(1,),
            in_specs=[ANY] * 4,
            out_specs=[ANY] * len(cuts),
            scratch_shapes=[
                pltpu.VMEM((F, 512), bf16),
                pltpu.VMEM((8, 512, 256), bf16),
                pltpu.VMEM((8 * F, 128), bf16),
                pltpu.VMEM((8, SLAB, 128), bf16),
                pltpu.VMEM((8, SLAB, 128), bf16),
                pltpu.SemaphoreType.DMA,
                pltpu.SemaphoreType.DMA((8,)),
                pltpu.SemaphoreType.DMA,
                pltpu.SemaphoreType.DMA((8,)),
            ],
        ),
        out_shape=[jax.ShapeDtypeStruct((n, SLAB, 128), bf16) for n in cuts],
        compiler_params=pltpu.CompilerParams(vmem_limit_bytes=VMEM),
        cost_estimate=cost(2 * 512 * F * 2048, 6 * MIB),
        name="packed",
    )(groups, table, left, right, got if added else right, ready)


def expand_kernel(turned, keep, table, w, f, out, s, dense):
    total = w[0].astype(f32) + f[0].astype(f32)
    s[0:SLAB, :] = total
    s[SLAB : 2 * SLAB, :] = pltpu.roll(total, 64, 1)
    target = dense if turned else out
    for r in range(16):
        rows = slice(r * B, (r + 1) * B)
        for c in range(4):
            row = pl.multiple_of(table[r * 4 + c], B)
            half = slice((c % 2) * B, (c % 2 + 1) * B)
            block = s[pl.ds(row, B), half]
            target[rows, c * B : (c + 1) * B] = jnp.where(keep[r * 4 + c] != 0, block, 0.0)
    if turned:
        for r in range(0, F, 128):
            for c in range(0, 256, 128):
                out[c : c + 128, r : r + 128] = dense[r : r + 128, c : c + 128].T


def expand(turned, keep, table, w, f):
    slab = pl.BlockSpec((1, SLAB, 128), lambda i, k, p: (0, 0, 0))
    shape = (256, F) if turned else (F, 256)
    return pl.pallas_call(
        functools.partial(expand_kernel, turned),
        grid_spec=pltpu.PrefetchScalarGridSpec(
            num_scalar_prefetch=2,
            grid=(1,),
            in_specs=[slab, slab],
            out_specs=pl.BlockSpec(shape, lambda i, k, p: (0, 0)),
            scratch_shapes=[pltpu.VMEM((2 * SLAB, 128), f32), pltpu.VMEM((F, 256), f32)],
        ),
        out_shape=jax.ShapeDtypeStruct(shape, f32),
        compiler_params=pltpu.CompilerParams(vmem_limit_bytes=VMEM),
        cost_estimate=cost(0, 2 * MIB),
        name="expand",
    )(keep, table, w, f)


def plan(mask_up, mask_down):
    up = mask_up.reshape(16, 4, 16).transpose(0, 2, 1).reshape(16, 64)
    down = mask_down.reshape(16, 16, 4).transpose(1, 0, 2).reshape(16, 64)
    keep = (jnp.stack([up, down]) != 0).astype(jnp.int32)
    place = jnp.arange(64, dtype=jnp.int32)
    slot = jnp.sum(keep[:, :, None, :] * (place[None, :] < place[:, None]), axis=-1)
    wanted = jnp.arange(KEPT, dtype=jnp.int32)
    hit = (slot[:, :, None, :] == wanted[:, None]) & (keep[:, :, None, :] != 0)
    here = (place // 4) * B + ((place % 4) // 2) * F
    turned = (place % 2) ^ (wanted[:, None] % 2)
    source = jnp.sum(jnp.where(hit, here + turned * (2 * F), 0), axis=-1)
    back = (slot // 2) * B + ((slot % 2) ^ (place % 2)) * SLAB
    return source, jnp.where(keep != 0, back, 0), keep


def add(*terms):
    total = terms[0].astype(f32)
    for term in terms[1:]:
        total = total + term.astype(f32)
    return total.astype(bf16)


def cat(*parts):
    return jnp.concatenate(parts, axis=0)


def stage(*values):
    return lax.optimization_barrier(values)


def local(tokens, w_up, w_down, mask_up, mask_down, cotangent):
    x, d = tokens, cotangent
    dp = lax.axis_index("dp")
    y, xh, c = dp // 4, (dp // 2) % 2, dp % 2

    xm, xp = shift(x, dz=1), shift(x, dz=-1)
    l1, r1 = shift(cat(x[:32], d[:32]), dx=1), shift(cat(x[32:], d[32:]), dx=-1)
    uk = kept_weight(w_up, mask_up)
    table, back, keep = plan(mask_up, mask_down)
    own = [lax.dynamic_index_in_dim(v, dp, 1, keepdims=False) for v in (keep, back)]

    xm, xp, l1, r1, uk, table = stage(xm, xp, l1, r1, uk, table)
    ea, eb = shift(cat(xm[:32], d), dz=1), shift(cat(xp[32:], d), dz=-1)
    l2, r2 = shift(cat(xm[:32], xp[:32]), dx=1), shift(cat(xm[32:], xp[32:]), dx=-1)
    dk = kept_weight(w_down, mask_down, xm)

    ea, eb, l2, r2, dk, *lists = stage(ea, eb, l2, r2, dk, *[v[k] for v in own for k in range(2)])
    keep_up, keep_down, back_up, back_down = lists
    l3 = shift(cat(ea[:32], ea[32:64], eb[32:64]), dx=1)
    r3 = shift(cat(eb[:32], ea[64:], eb[64:]), dx=-1)
    fa, fb = shift(ea[32:64], dz=1), shift(eb[64:], dz=-1)
    half = hidden_of(0, TOKENS_COLUMN, [x, xm, xp, ea, eb], uk, l2)
    (o_col,) = share(False, half[1], 0, (256,), dk, half[1])

    fa, fb, l3, r3, o_col = stage(fa, fb, l3, r3, o_col)
    l4, r4 = shift(fa, dx=1), shift(fb, dx=-1)
    pre, hid, hid_t, xs = hidden_of(1, TOKENS_SIDE, [l1, l2, l3, r1, r2, r3], uk, o_col, half)
    o_left, o_right = share(False, hid, 1, (128, 128), dk, xs)

    oa, ob = shift(o_left, dx=-1), shift(o_right, dx=1)
    gp, gp_t, ds = grad_pre_of([d, ea, eb, fa, fb, l1, l3, l4, r1, r3, r4], dk, pre, o_left)

    pair, mirror = y ^ 1, 3 - y
    pairs = [(3 - pair, 0), (pair, 0), (mirror ^ 1, 1), (mirror, 1), (mirror, 0), (y, 0), (pair, 1), (y, 1)]
    near = jnp.stack([4 * at + (xh ^ e) * 2 + c for at, e in pairs]).astype(jnp.int32)
    away = near ^ 1
    cuts = (2, 2, 2, 2)

    (up_away,) = packed(away, table[0], gp_t, xs, gp)
    up_got = to_core(up_away)
    t_col, t_left, t_right = share(True, gp, 0, (256, 128, 128), uk, up_away)

    oa, ob, t_col, t_left, t_right = stage(oa, ob, t_col, t_left, t_right)
    ta, tb = shift(t_left, dx=-1), shift(t_right, dx=1)
    (down_away,) = packed(away, table[1], hid_t, ds, t_col)
    down_got = to_core(down_away)
    ua, ub, uc, ud = packed(near, table[0], gp_t, xs, down_away, cuts, up_got)
    u1, u2 = to_pair(ua), to_mirror(ub)
    da, db, dc, dd = packed(near, table[1], hid_t, ds, ud, cuts, down_got)

    ta, tb, dd = stage(ta, tb, dd)
    o, t, a, b, g, h = o_col, t_col, oa, ob, ta, tb
    za, zb = row_sums(
        [
            [[(o, 192), (a, 96)], [(t, 192), (g, 96)]],
            [[(o, 224), (b, 96)], [(t, 224), (h, 96)]],
        ],
        dd,
    )
    da, db, za, zb = stage(da, db, za, zb)
    za, zb = shift(za, dz=1), shift(zb, dz=-1)
    d1, d2 = to_pair(da), to_mirror(db)
    u3, u4 = stage(add(uc[0:1], u1[0:1]), add(ud[0:1], u2[0:1]))

    p, m = row_sums(
        [
            [[(o, 128), (a, 64), (za, 0)], [(o, 160), (b, 64)], [(t, 128), (g, 64), (za, 32)], [(t, 160), (h, 64)]],
            [[(o, 64), (a, 32)], [(o, 96), (b, 32), (zb, 0)], [(t, 64), (g, 32)], [(t, 96), (h, 32), (zb, 32)]],
        ],
        u4,
    )
    u3, u4, p, m = stage(u3, u4, p, m)
    p, m = shift(p, dz=1), shift(m, dz=-1)
    u3, u4 = to_mirror(u3), to_pair(u4)
    d1, d2, dc, _ = stage(d1, d2, dc, u1)
    d3, d4 = to_mirror(add(dc[0:1], d1[0:1])), to_pair(add(dd[0:1], d2[0:1]))

    u3, u4, dc = stage(u3, u4, dc)
    up_far = shift(add(ud[1:2], u2[1:2], u4), dx=2)
    up_near = add(uc[1:2], u1[1:2], u3)
    grad_up = expand(True, keep_up, back_up, up_near, up_far)

    down_far = shift(add(dd[1:2], d2[1:2], d4), dx=2)
    down_near = add(dc[1:2], d1[1:2], d3)
    output, grad_tokens = row_sums(
        [
            [[(o, 0), (a, 0), (p, 0), (m, 0)], [(o, 32), (b, 0), (p, 32), (m, 32)]],
            [[(t, 0), (g, 0), (p, 64), (m, 64)], [(t, 32), (h, 0), (p, 96), (m, 96)]],
        ],
        up_near,
    )
    output, down_near = stage(output, down_near)
    grad_down = expand(False, keep_down, back_down, down_near, down_far)
    return output, grad_tokens, grad_up, grad_down


def solution(mesh):
    placed = (
        P(("dp", "tensor"), None),
        P(None, "tensor"),
        P("tensor", None),
        P(None, "tensor"),
        P("tensor", None),
        P(("dp", "tensor"), None),
    )
    return jax.shard_map(
        local,
        mesh=mesh,
        in_specs=placed,
        out_specs=(
            P(("dp", "tensor"), None),
            P(("dp", "tensor"), None),
            P("dp", "tensor"),
            P("tensor", "dp"),
        ),
        check_vma=False,
    )
```

```python
import functools
import math

import jax
import jax.numpy as jnp
from jax import lax
from jax.experimental import pallas as pl
from jax.experimental.pallas import tpu as pltpu
from jax.sharding import PartitionSpec as P

B = 64
D = 4096
F = 1024
KEPT = 40
SLAB = KEPT // 2 * B
MIB = 1 << 20
VMEM = 60 * MIB
C = math.sqrt(2.0 / math.pi)
f32, bf16 = jnp.float32, jnp.bfloat16
AXES = ("dp", "tensor")


def device_at(x, y, z, c):
    x, y, z = x % 4, y % 4, z % 4
    return ((y * 2 + x // 2) * 2 + c) * 8 + z * 2 + x % 2


def send(value, to):
    pairs = [
        (device_at(x, y, z, c), device_at(*to(x, y, z, c)))
        for x in range(4)
        for y in range(4)
        for z in range(4)
        for c in range(2)
    ]
    return lax.ppermute(value, AXES, pairs)


def shift(value, dx=0, dz=0):
    return send(value, lambda x, y, z, c: (x + dx, y, z + dz, c))


def to_core(value):
    return send(value, lambda x, y, z, c: (x, y, z, 1 - c))


def to_pair(value):
    return send(value, lambda x, y, z, c: (x, y ^ 1, z, c))


def to_mirror(value):
    return send(value, lambda x, y, z, c: (x, 3 - y, z, c))


def cost(flops, nbytes):
    return pl.CostEstimate(flops=int(flops) * 64, bytes_accessed=int(nbytes) * 64, transcendentals=0)


def spread(blocks):
    row = lax.broadcasted_iota(jnp.int32, (blocks, blocks * B), 0)
    col = lax.broadcasted_iota(jnp.int32, (blocks, blocks * B), 1)
    return (row == col // B).astype(f32).astype(bf16)


def mask_kernel(blocks, per, mask, w, *rest):
    kept, rows = rest[-2:]
    i = pl.program_id(0)

    @pl.when(i == 0)
    def _():
        rows[...] = jnp.dot(
            mask[...].astype(f32).astype(bf16), spread(blocks), preferred_element_type=f32
        )

    for k in range(per):
        at = slice(k * B, (k + 1) * B)
        kept[at, :] = (w[at, :].astype(f32) * rows[pl.ds(per * i + k, 1), :]).astype(bf16)


def kept_weight(w, mask, *ready):
    rows, cols = w.shape
    steps = 4
    block = pl.BlockSpec((rows // steps, cols), lambda i: (i, 0))
    return pl.pallas_call(
        functools.partial(mask_kernel, cols // B, rows // B // steps),
        grid=(steps,),
        in_specs=[pl.BlockSpec(mask.shape, lambda i: (0, 0)), block]
        + [pl.BlockSpec(memory_space=pl.ANY)] * len(ready),
        out_specs=block,
        out_shape=jax.ShapeDtypeStruct((rows, cols), bf16),
        scratch_shapes=[pltpu.VMEM((rows // B, cols), f32)],
        compiler_params=pltpu.CompilerParams(vmem_limit_bytes=VMEM),
        cost_estimate=cost(0, 18 * MIB),
        name="kept_weight",
    )(mask, w, *ready)


TOKENS_COLUMN = ((0, 0, 64, 0), (1, 0, 64, 64), (2, 0, 64, 128), (3, 0, 32, 192), (4, 0, 32, 224))
TOKENS_SIDE = tuple(
    (3 * s + p, 0, n, 128 * s + dst) for s in range(2) for p, n, dst in ((0, 32, 0), (1, 64, 32), (2, 32, 96))
)
COTANGENTS = (
    (0, 0, 64, 0),
    (1, 32, 64, 64),
    (2, 32, 64, 128),
    (3, 0, 32, 192),
    (4, 0, 32, 224),
    (5, 32, 32, 256),
    (6, 32, 64, 288),
    (7, 0, 32, 352),
    (8, 32, 32, 384),
    (9, 32, 64, 416),
    (10, 0, 32, 480),
)
ANY = pl.BlockSpec(memory_space=pl.ANY)


def collect(table, pieces, rows, sem, out, row, out_sem):
    i = pl.program_id(0)
    keep = pltpu.make_async_copy(rows, out.at[pl.ds(row, rows.shape[0]), :], out_sem)

    @pl.when(i == 0)
    def _():
        moves = [
            pltpu.make_async_copy(pieces[p].at[pl.ds(src, n), :], rows.at[pl.ds(dst, n), :], sem.at[k])
            for k, (p, src, n, dst) in enumerate(table)
        ]
        for move in moves:
            move.start()
        for move in moves:
            move.wait()
        keep.start()

    def finish():
        @pl.when(i == pl.num_programs(0) - 1)
        def _():
            keep.wait()

    return finish


def hidden_kernel(table, n_pieces, half, *refs):
    pieces, uk = refs[:n_pieces], refs[n_pieces]
    pre_out, hid, hid_t, x_out, xs, sem, out_sem = refs[-7:]
    finish = collect(table, pieces, xs, sem, x_out, 256 * half, out_sem)
    pre = jnp.dot(xs[...], uk[...], preferred_element_type=f32)
    pre_out[...] = pre
    h = pre * (0.5 + 0.5 * jnp.tanh(pre * (C + C * 0.044715 * (pre * pre))))
    hid[...] = h.astype(bf16)
    hid_t[...] = h.T.astype(bf16)
    finish()


def hidden_of(half, table, pieces, up_kept, ready, earlier=()):
    n, tile = len(pieces), 512
    across = pl.BlockSpec((256, tile), lambda i: (half, i))
    return pl.pallas_call(
        functools.partial(hidden_kernel, table, n, half),
        grid=(F // tile,),
        in_specs=[ANY] * n
        + [pl.BlockSpec((D, tile), lambda i: (0, i)), ANY]
        + [ANY] * len(earlier),
        out_specs=[across, across, pl.BlockSpec((tile, 256), lambda i: (i, half)), ANY],
        out_shape=[
            jax.ShapeDtypeStruct((512, F), f32),
            jax.ShapeDtypeStruct((512, F), bf16),
            jax.ShapeDtypeStruct((F, 512), bf16),
            jax.ShapeDtypeStruct((512, D), bf16),
        ],
        input_output_aliases={n + 2 + k: k for k in range(len(earlier))},
        scratch_shapes=[
            pltpu.VMEM((256, D), bf16),
            pltpu.SemaphoreType.DMA((len(table),)),
            pltpu.SemaphoreType.DMA,
        ],
        compiler_params=pltpu.CompilerParams(vmem_limit_bytes=VMEM),
        cost_estimate=cost(2 * 256 * D * F, 14 * MIB),
        name="hidden",
    )(*pieces, up_kept, ready, *earlier)


def back_kernel(table, n_pieces, *refs):
    pieces, (dk, pre_ref) = refs[:n_pieces], refs[n_pieces : n_pieces + 2]
    gp, gp_t, d_out, ds, sem, out_sem = refs[-6:]
    finish = collect(table, pieces, ds, sem, d_out, 0, out_sem)
    back = lax.dot_general(ds[...], dk[...], (((1,), (1,)), ((), ())), preferred_element_type=f32)
    pre = pre_ref[...]
    square = pre * pre
    s = 0.5 + 0.5 * jnp.tanh(pre * (C + C * 0.044715 * square))
    g = back * (s + pre * s * (1.0 - s) * (2.0 * C + 6.0 * C * 0.044715 * square))
    gp[...] = g.astype(bf16)
    gp_t[...] = g.T.astype(bf16)
    finish()


def grad_pre_of(pieces, down_kept, pre, ready):
    n, tile = len(pieces), 256
    return pl.pallas_call(
        functools.partial(back_kernel, COTANGENTS, n),
        grid=(F // tile,),
        in_specs=[ANY] * n
        + [
            pl.BlockSpec((tile, D), lambda i: (i, 0)),
            pl.BlockSpec((512, tile), lambda i: (0, i)),
            ANY,
        ],
        out_specs=[
            pl.BlockSpec((512, tile), lambda i: (0, i)),
            pl.BlockSpec((tile, 512), lambda i: (i, 0)),
            ANY,
        ],
        out_shape=[
            jax.ShapeDtypeStruct((512, F), bf16),
            jax.ShapeDtypeStruct((F, 512), bf16),
            jax.ShapeDtypeStruct((512, D), bf16),
        ],
        scratch_shapes=[
            pltpu.VMEM((512, D), bf16),
            pltpu.SemaphoreType.DMA((len(COTANGENTS),)),
            pltpu.SemaphoreType.DMA,
        ],
        compiler_params=pltpu.CompilerParams(vmem_limit_bytes=VMEM),
        cost_estimate=cost(2 * 512 * D * F, 20 * MIB),
        name="grad_pre",
    )(*pieces, down_kept, pre, ready)


def share_kernel(turned, cuts, left, w, _, *outs):
    dims = (((1,), (1 if turned else 0,)), ((), ()))
    total = lax.dot_general(left[...], w[...], dims, preferred_element_type=f32).astype(bf16)
    row = 0
    for out, rows in zip(outs, cuts):
        out[...] = total[row : row + rows, :]
        row += rows


def share(turned, left, block, cuts, w, ready):
    m, tile = sum(cuts), 1024
    return pl.pallas_call(
        functools.partial(share_kernel, turned, cuts),
        grid=(D // tile,),
        in_specs=[
            pl.BlockSpec((m, F), lambda i: (block, 0)),
            pl.BlockSpec((tile, F), lambda i: (i, 0)) if turned else pl.BlockSpec((F, tile), lambda i: (0, i)),
            ANY,
        ],
        out_specs=[pl.BlockSpec((rows, tile), lambda i: (0, i)) for rows in cuts],
        out_shape=[jax.ShapeDtypeStruct((rows, D), bf16) for rows in cuts],
        compiler_params=pltpu.CompilerParams(vmem_limit_bytes=VMEM),
        cost_estimate=cost(2 * m * D * F, 12 * MIB),
        name="share",
    )(left, w, ready)


def row_sums_kernel(plan, n, *refs):
    for out, segments in zip(refs[n + 1 :], plan):
        for k, terms in enumerate(segments):
            total = refs[terms[0]][...].astype(f32)
            for term in terms[1:]:
                total = total + refs[term][...].astype(f32)
            out[32 * k : 32 * (k + 1), :] = total.astype(bf16)


def row_sums(outs, ready):
    arrays, specs, plan = [], [], []
    tile = D // 2
    for segments in outs:
        plan.append([])
        for terms in segments:
            plan[-1].append(range(len(arrays), len(arrays) + len(terms)))
            for array, row in terms:
                arrays.append(array)
                specs.append(pl.BlockSpec((32, tile), lambda i, at=row // 32: (at, i)))
    return pl.pallas_call(
        functools.partial(row_sums_kernel, plan, len(arrays)),
        grid=(D // tile,),
        in_specs=specs + [ANY],
        out_specs=[pl.BlockSpec((32 * len(segments), tile), lambda i: (0, i)) for segments in outs],
        out_shape=[jax.ShapeDtypeStruct((32 * len(segments), D), bf16) for segments in outs],
        compiler_params=pltpu.CompilerParams(vmem_limit_bytes=VMEM),
        cost_estimate=cost(0, 3 * MIB),
        name="row_sums",
    )(*arrays, ready)


def packed_kernel(cuts, added, groups, table, left, right, got, _, *refs):
    outs, (a, b, t, buf, add_buf, a_sem, b_sem, got_sem, out_sem) = refs[: len(cuts)], refs[len(cuts) :]
    first = pltpu.make_async_copy(left, a, a_sem)
    first.start()
    rights = []
    for q in range(8):
        col = pl.multiple_of(groups[q] * 256, 256)
        rights.append(pltpu.make_async_copy(right.at[:, pl.ds(col, 256)], b.at[q], b_sem.at[q]))
        rights[q].start()
    if added:
        more = pltpu.make_async_copy(got, add_buf, got_sem)
        more.start()
    places = [(out, k) for out, n in zip(outs, cuts) for k in range(n)]
    moves = [
        pltpu.make_async_copy(buf.at[q], out.at[k], out_sem.at[q]) for q, (out, k) in enumerate(places)
    ]
    first.wait()
    for q in range(8):
        j = groups[q]
        rights[q].wait()
        base = (q % 2) * 4 * F
        for r in range(0, F, 256):
            acc = jnp.dot(a[r : r + 256, :], b[q], preferred_element_type=f32)
            for ct in range(2):
                part = acc[:, ct * 128 : (ct + 1) * 128]
                row = base + ct * F + r
                t[row : row + 256, :] = part.astype(bf16)
                row += 2 * F
                t[row : row + 256, :] = pltpu.roll(part, 64, 1).astype(bf16)
        for p in range(KEPT // 2):
            ra = pl.multiple_of(base + table[j, 2 * p], B)
            rb = pl.multiple_of(base + table[j, 2 * p + 1], B)
            to = slice(p * B, (p + 1) * B)
            buf[q, to, 0:B] = t[pl.ds(ra, B), 0:B]
            buf[q, to, B : 2 * B] = t[pl.ds(rb, B), B : 2 * B]
        if added:
            if q == 0:
                more.wait()
            buf[q] = (buf[q].astype(f32) + add_buf[q].astype(f32)).astype(bf16)
        moves[q].start()
    for move in moves:
        move.wait()


def packed(groups, table, left, right, ready, cuts=(8,), got=None):
    added = got is not None
    return pl.pallas_call(
        functools.partial(packed_kernel, cuts, added),
        grid_spec=pltpu.PrefetchScalarGridSpec(
            num_scalar_prefetch=2,
            grid=(1,),
            in_specs=[ANY] * 4,
            out_specs=[ANY] * len(cuts),
            scratch_shapes=[
                pltpu.VMEM((F, 512), bf16),
                pltpu.VMEM((8, 512, 256), bf16),
                pltpu.VMEM((8 * F, 128), bf16),
                pltpu.VMEM((8, SLAB, 128), bf16),
                pltpu.VMEM((8, SLAB, 128), bf16),
                pltpu.SemaphoreType.DMA,
                pltpu.SemaphoreType.DMA((8,)),
                pltpu.SemaphoreType.DMA,
                pltpu.SemaphoreType.DMA((8,)),
            ],
        ),
        out_shape=[jax.ShapeDtypeStruct((n, SLAB, 128), bf16) for n in cuts],
        compiler_params=pltpu.CompilerParams(vmem_limit_bytes=VMEM),
        cost_estimate=cost(2 * 512 * F * 2048, 6 * MIB),
        name="packed",
    )(groups, table, left, right, got if added else right, ready)


def expand_kernel(turned, keep, table, w, f, out, s, dense):
    total = w[0].astype(f32) + f[0].astype(f32)
    s[0:SLAB, :] = total
    s[SLAB : 2 * SLAB, :] = pltpu.roll(total, 64, 1)
    target = dense if turned else out
    for r in range(16):
        rows = slice(r * B, (r + 1) * B)
        for c in range(4):
            row = pl.multiple_of(table[r * 4 + c], B)
            half = slice((c % 2) * B, (c % 2 + 1) * B)
            block = s[pl.ds(row, B), half]
            target[rows, c * B : (c + 1) * B] = jnp.where(keep[r * 4 + c] != 0, block, 0.0)
    if turned:
        for r in range(0, F, 128):
            for c in range(0, 256, 128):
                out[c : c + 128, r : r + 128] = dense[r : r + 128, c : c + 128].T


def expand(turned, keep, table, w, f):
    slab = pl.BlockSpec((1, SLAB, 128), lambda i, k, p: (0, 0, 0))
    shape = (256, F) if turned else (F, 256)
    return pl.pallas_call(
        functools.partial(expand_kernel, turned),
        grid_spec=pltpu.PrefetchScalarGridSpec(
            num_scalar_prefetch=2,
            grid=(1,),
            in_specs=[slab, slab],
            out_specs=pl.BlockSpec(shape, lambda i, k, p: (0, 0)),
            scratch_shapes=[pltpu.VMEM((2 * SLAB, 128), f32), pltpu.VMEM((F, 256), f32)],
        ),
        out_shape=jax.ShapeDtypeStruct(shape, f32),
        compiler_params=pltpu.CompilerParams(vmem_limit_bytes=VMEM),
        cost_estimate=cost(0, 2 * MIB),
        name="expand",
    )(keep, table, w, f)


def plan(mask_up, mask_down):
    up = mask_up.reshape(16, 4, 16).transpose(0, 2, 1).reshape(16, 64)
    down = mask_down.reshape(16, 16, 4).transpose(1, 0, 2).reshape(16, 64)
    keep = (jnp.stack([up, down]) != 0).astype(jnp.int32)
    place = jnp.arange(64, dtype=jnp.int32)
    slot = jnp.sum(keep[:, :, None, :] * (place[None, :] < place[:, None]), axis=-1)
    wanted = jnp.arange(KEPT, dtype=jnp.int32)
    hit = (slot[:, :, None, :] == wanted[:, None]) & (keep[:, :, None, :] != 0)
    here = (place // 4) * B + ((place % 4) // 2) * F
    turned = (place % 2) ^ (wanted[:, None] % 2)
    source = jnp.sum(jnp.where(hit, here + turned * (2 * F), 0), axis=-1)
    back = (slot // 2) * B + ((slot % 2) ^ (place % 2)) * SLAB
    return source, jnp.where(keep != 0, back, 0), keep


def add(*terms):
    total = terms[0].astype(f32)
    for term in terms[1:]:
        total = total + term.astype(f32)
    return total.astype(bf16)


def cat(*parts):
    return jnp.concatenate(parts, axis=0)


def stage(*values):
    return lax.optimization_barrier(values)


def local(tokens, w_up, w_down, mask_up, mask_down, cotangent):
    x, d = tokens, cotangent
    dp = lax.axis_index("dp")
    y, xh, c = dp // 4, (dp // 2) % 2, dp % 2

    xm, xp = shift(x, dz=1), shift(x, dz=-1)
    l1, r1 = shift(cat(x[:32], d[:32]), dx=1), shift(cat(x[32:], d[32:]), dx=-1)
    uk = kept_weight(w_up, mask_up)
    table, back, keep = plan(mask_up, mask_down)
    own = [lax.dynamic_index_in_dim(v, dp, 1, keepdims=False) for v in (keep, back)]

    xm, xp, l1, r1, uk, table = stage(xm, xp, l1, r1, uk, table)
    ea, eb = shift(cat(xm[:32], d), dz=1), shift(cat(xp[32:], d), dz=-1)
    l2, r2 = shift(cat(xm[:32], xp[:32]), dx=1), shift(cat(xm[32:], xp[32:]), dx=-1)
    dk = kept_weight(w_down, mask_down, xm)

    ea, eb, l2, r2, dk, *lists = stage(ea, eb, l2, r2, dk, *[v[k] for v in own for k in range(2)])
    keep_up, keep_down, back_up, back_down = lists
    l3 = shift(cat(ea[:32], ea[32:64], eb[32:64]), dx=1)
    r3 = shift(cat(eb[:32], ea[64:], eb[64:]), dx=-1)
    fa, fb = shift(ea[32:64], dz=1), shift(eb[64:], dz=-1)
    half = hidden_of(0, TOKENS_COLUMN, [x, xm, xp, ea, eb], uk, l2)
    (o_col,) = share(False, half[1], 0, (256,), dk, half[1])

    fa, fb, l3, r3, o_col = stage(fa, fb, l3, r3, o_col)
    l4, r4 = shift(fa, dx=1), shift(fb, dx=-1)
    pre, hid, hid_t, xs = hidden_of(1, TOKENS_SIDE, [l1, l2, l3, r1, r2, r3], uk, o_col, half)
    o_left, o_right = share(False, hid, 1, (128, 128), dk, xs)

    oa, ob = shift(o_left, dx=-1), shift(o_right, dx=1)
    gp, gp_t, ds = grad_pre_of([d, ea, eb, fa, fb, l1, l3, l4, r1, r3, r4], dk, pre, o_left)

    pair, mirror = y ^ 1, 3 - y
    pairs = [(3 - pair, 0), (pair, 0), (mirror ^ 1, 1), (mirror, 1), (mirror, 0), (y, 0), (pair, 1), (y, 1)]
    near = jnp.stack([4 * at + (xh ^ e) * 2 + c for at, e in pairs]).astype(jnp.int32)
    away = near ^ 1
    cuts = (2, 2, 2, 2)

    (up_away,) = packed(away, table[0], gp_t, xs, gp)
    up_got = to_core(up_away)
    t_col, t_left, t_right = share(True, gp, 0, (256, 128, 128), uk, up_away)

    oa, ob, t_col, t_left, t_right = stage(oa, ob, t_col, t_left, t_right)
    ta, tb = shift(t_left, dx=-1), shift(t_right, dx=1)
    (down_away,) = packed(away, table[1], hid_t, ds, t_col)
    down_got = to_core(down_away)
    ua, ub, uc, ud = packed(near, table[0], gp_t, xs, down_away, cuts, up_got)
    u1, u2 = to_pair(ua), to_mirror(ub)
    da, db, dc, dd = packed(near, table[1], hid_t, ds, ud, cuts, down_got)

    ta, tb, dd = stage(ta, tb, dd)
    o, t, a, b, g, h = o_col, t_col, oa, ob, ta, tb
    za, zb = row_sums(
        [
            [[(o, 192), (a, 96)], [(t, 192), (g, 96)]],
            [[(o, 224), (b, 96)], [(t, 224), (h, 96)]],
        ],
        dd,
    )
    da, db, za, zb = stage(da, db, za, zb)
    za, zb = shift(za, dz=1), shift(zb, dz=-1)
    d1, d2 = to_pair(da), to_mirror(db)
    u3, u4 = stage(add(uc[0:1], u1[0:1]), add(ud[0:1], u2[0:1]))

    p, m = row_sums(
        [
            [[(o, 128), (a, 64), (za, 0)], [(o, 160), (b, 64)], [(t, 128), (g, 64), (za, 32)], [(t, 160), (h, 64)]],
            [[(o, 64), (a, 32)], [(o, 96), (b, 32), (zb, 0)], [(t, 64), (g, 32)], [(t, 96), (h, 32), (zb, 32)]],
        ],
        u4,
    )
    u3, u4, p, m = stage(u3, u4, p, m)
    p, m = shift(p, dz=1), shift(m, dz=-1)
    u3, u4 = to_mirror(u3), to_pair(u4)
    d1, d2, dc, _ = stage(d1, d2, dc, u1)
    d3, d4 = to_mirror(add(dc[0:1], d1[0:1])), to_pair(add(dd[0:1], d2[0:1]))

    u3, u4, dc = stage(u3, u4, dc)
    up_far = shift(add(ud[1:2], u2[1:2], u4), dx=2)
    up_near = add(uc[1:2], u1[1:2], u3)
    grad_up = expand(True, keep_up, back_up, up_near, up_far)

    down_far = shift(add(dd[1:2], d2[1:2], d4), dx=2)
    down_near = add(dc[1:2], d1[1:2], d3)
    grad_down = expand(False, keep_down, back_down, down_near, down_far)
    output, grad_tokens = row_sums(
        [
            [[(o, 0), (a, 0), (p, 0), (m, 0)], [(o, 32), (b, 0), (p, 32), (m, 32)]],
            [[(t, 0), (g, 0), (p, 64), (m, 64)], [(t, 32), (h, 0), (p, 96), (m, 96)]],
        ],
        grad_down,
    )
    return output, grad_tokens, grad_up, grad_down


def solution(mesh):
    placed = (
        P(("dp", "tensor"), None),
        P(None, "tensor"),
        P("tensor", None),
        P(None, "tensor"),
        P("tensor", None),
        P(("dp", "tensor"), None),
    )
    return jax.shard_map(
        local,
        mesh=mesh,
        in_specs=placed,
        out_specs=(
            P(("dp", "tensor"), None),
            P(("dp", "tensor"), None),
            P("dp", "tensor"),
            P("tensor", "dp"),
        ),
        check_vma=False,
    )
```
